256 devices in a mesh: seq: 8 (over z_lo, y), frm: 32 (over x, z_hi, core).
Axes of the slice: x: 4, y: 4, z: 8 (z_hi: 4, z_lo: 2; z = z_hi * 2 + z_lo), core: 2. Of those that a mesh axis runs over, the one named last changes fastest.
Arguments:
- queries: bfloat16 [64, 128, 5120], P('frm', 'seq'), may hold values from -26.4 to 26.4
- keys: bfloat16 [64, 128, 5120], P('frm', 'seq'), may hold values from -8.4 to 8.4
- values: bfloat16 [64, 128, 5120], P('frm', 'seq'), may hold values from -6 to 6
- clip_ids: int32 [64], replicated, may hold values from 0 to 4, never falling along the last dimension, each value on 1 to 33 neighbouring positions
- w_head: bfloat16 [5120, 64], replicated, may hold values from -1 to 1
- b_head: float32 [64], replicated, may hold values from -3 to 3
- w_in: bfloat16 [432, 384], replicated, may hold values from -0.3125 to 0.3125
- b_in: float32 [384], replicated, may hold values from -3 to 3
- gain_in: float32 [384], replicated, may hold values from 0.25 to 1.75
- w_up: bfloat16 [3456, 192], replicated, may hold values from -0.109375 to 0.109375
- b_up: float32 [192], replicated, may hold values from -3 to 3
Outputs:
- decoded: bfloat16 [64, 32, 12288], P('frm', 'seq')
The draws below stay inside these ranges and needn't reach their ends.
Inputs may be any that keep to these rules, and one draw needn't show every extreme that they name: `clip_ids`: frames of one clip are consecutive and clip numbers never fall; every clip has 1 to 33 frames and one has exactly 33.
All inputs are finite; a program needn't handle non-finite values.
Results may differ from the reference program's by a relative error of at most 0.014.
Values may be sent and summed in bfloat16 or wider, within the bound.
No kernel may reach another device: no remote copies, remote signals or barrier semaphores. Data moves between devices by JAX's collectives and lax.ppermute only.
A program may use at most 128 MiB of HBM per device.

```python
import math
import jax
import jax.numpy as jnp
import numpy as np
from jax import lax

HEADS = 40
HD = 128
LC = 16
C1 = 384
CO = 192
PW = 16
CLIPS = 5
D = 5120
PH = 8
FTOK = 128
FRAMES = 64
CLIP_MAX = 33
TOKENS = 8192


def draw_keys(key, part):
    key = jax.random.fold_in(key, 11)
    keyed = jnp.clip(1.4 * jax.random.normal(key, (TOKENS, D), jnp.float32), -8.4, 8.4)
    return keyed.reshape(FRAMES, FTOK, D).astype(jnp.bfloat16)


def draw_queries(key, part):
    key = jax.random.fold_in(key, 12)
    drawn = jnp.clip(1.4 * jax.random.normal(key, (TOKENS, D), jnp.float32), -8.4, 8.4)
    return drawn.reshape(FRAMES, FTOK, D).astype(jnp.bfloat16)


def shard_levels(own_key, shape, cuts, low, top_value):
    factor_of, own = 1.0, jax.random.fold_in(own_key, 6)
    for dim, shards_of in cuts:
        draws = jnp.exp(jax.random.uniform(jax.random.fold_in(own, dim), (shards_of,), jnp.float32, low / len(cuts), top_value / len(cuts)))
        factor_of = factor_of * jnp.repeat(draws, shape[dim] // shards_of).reshape([-1 if axis == dim else 1 for axis in range(len(shape))])
    return factor_of


def profile(number_of, total, reach, slope):
    weights = [(1 << 20) // math.isqrt(standing ** slope) + 1 for standing in range(2, number_of + 1)]
    surplus, given = total - reach - (number_of - 1), [1] * (number_of - 1)
    while surplus > 0:
        free = [i for i in range(number_of - 1) if given[i] < reach]
        mass, left = sum([weights[i] for i in free]), surplus
        for i in free:
            addition = min(reach - given[i], max(1, left * weights[i] // mass), surplus)
            given[i] = given[i] + addition
            surplus = surplus - addition
    return np.array([reach] + given)


def uneven(own_key, amount, total, reach, lean):
    if amount == 2:
        one = jax.random.randint(own_key, (), max(1, total - reach), min(reach, total - 1) + 1)
        return jnp.stack([one, total - one])
    tallies = jnp.asarray(profile(amount, total, reach, lean), jnp.int32)
    twos = (amount - 1) // 2
    donor, sink = tallies[1:1 + 2 * twos:2], tallies[2:2 + 2 * twos:2]
    room = jnp.minimum(donor - 1, reach - sink)
    moved = jax.random.randint(jax.random.fold_in(own_key, 1), (twos,), 0, 1 << 20) % (room + 1)
    tallies = tallies.at[1:1 + 2 * twos:2].set(donor - moved).at[2:2 + 2 * twos:2].set(sink + moved)
    return tallies[jax.random.permutation(jax.random.fold_in(own_key, 2), amount)]


def centred(rng, shape, width, bound, pieces=(), kind=jnp.bfloat16):
    gain = shard_levels(rng, shape, pieces, -0.22, 0.18) if pieces else 1.0
    values = jax.random.normal(rng, shape, jnp.float32) * width * gain
    return jnp.minimum(jnp.maximum(values, -bound), bound).astype(kind)


def setup_inputs(seed: int = 0) -> dict:
    key_list = jax.random.split(jax.random.key(seed), 12)
    queries = draw_queries(jax.random.fold_in(key_list[11], 71), 0)
    keys = draw_keys(jax.random.fold_in(key_list[11], 71), 0)
    values = centred(key_list[2], (FRAMES, FTOK, D), 1.0, 6.0, ((0, 32), (1, 8)))
    clip_ids = jnp.searchsorted(jnp.cumsum(uneven(key_list[3], CLIPS, FRAMES, CLIP_MAX, 1)), jnp.arange(FRAMES), side="right").astype(jnp.int32)
    w_head = centred(key_list[4], (D, 4 * LC), (max(D // 144, 1)) ** -0.5, 1.0)
    b_head = centred(key_list[5], (4 * LC,), 0.5, 3.0, (), jnp.float32)
    w_in = centred(key_list[6], (27 * LC, C1), (27 * LC) ** -0.5, 0.3125)
    b_in = centred(key_list[7], (C1,), 0.5, 3.0, (), jnp.float32)
    gain_in = jnp.clip(1.0 + 0.15 * jax.random.normal(key_list[8], (C1,), jnp.float32), 0.25, 1.75)
    w_up = centred(key_list[9], (9 * C1, CO), (9 * C1) ** -0.5, 0.109375)
    b_up = centred(key_list[10], (CO,), 0.5, 3.0, (), jnp.float32)
    return dict(queries=queries, keys=keys, values=values, clip_ids=clip_ids, w_head=w_head, b_head=b_head, w_in=w_in, b_in=b_in, gain_in=gain_in, w_up=w_up, b_up=b_up)


def reference(queries, keys, values, clip_ids, w_head, b_head, w_in, b_in, gain_in, w_up, b_up):
    flat_q = queries.reshape(TOKENS, HEADS, HD)
    flat_k = keys.reshape(TOKENS, HEADS, HD)
    flat_v = values.reshape(TOKENS, HEADS, HD)
    tok_clip = jnp.repeat(clip_ids, FTOK)
    block_rows = math.gcd(TOKENS, 512)
    score_scale = 1.0 / math.sqrt(HD)

    def one_head(head_index):
        query_head = lax.dynamic_index_in_dim(flat_q, head_index, 1, keepdims=False)
        key_head = lax.dynamic_index_in_dim(flat_k, head_index, 1, keepdims=False)
        value_head = lax.dynamic_index_in_dim(flat_v, head_index, 1, keepdims=False)

        def one_block(start_row):
            query_rows = lax.dynamic_slice_in_dim(query_head, start_row, block_rows, 0)
            clip_rows = lax.dynamic_slice_in_dim(tok_clip, start_row, block_rows, 0)
            scores = jnp.dot(query_rows, key_head.T, preferred_element_type=jnp.float32) * score_scale
            same_clip = clip_rows[:, None] == tok_clip[None, :]
            row_top = lax.optimization_barrier(jnp.max(jnp.where(same_clip, scores, -1e+30), axis=1, keepdims=True))
            weights = jnp.where(same_clip, jnp.exp(scores - row_top), 0.0)
            row_total = lax.optimization_barrier(jnp.sum(weights, axis=1, keepdims=True))
            mixed = jnp.dot(weights.astype(jnp.bfloat16), value_head, preferred_element_type=jnp.float32)
            return (mixed / row_total).astype(jnp.bfloat16)
        starts = jnp.arange(TOKENS // block_rows, dtype=jnp.int32) * block_rows
        return lax.map(one_block, starts).reshape(TOKENS, HD)
    heads_done = lax.map(one_head, jnp.arange(HEADS, dtype=jnp.int32))
    attended = jnp.transpose(heads_done, (1, 0, 2)).reshape(TOKENS, D)
    latent = (jnp.dot(attended, w_head, preferred_element_type=jnp.float32) + b_head).astype(jnp.bfloat16)
    latent_grid = latent.reshape(FRAMES, PH, PW, 2, 2, LC).transpose(0, 1, 3, 2, 4, 5).reshape(FRAMES, 2 * PH, 2 * PW, LC)
    padded = jnp.pad(latent_grid, ((2, 0), (1, 1), (1, 1), (0, 0)))
    clip_padded = jnp.concatenate([jnp.full((2,), -1, jnp.int32), clip_ids.astype(jnp.int32)])
    tap_list = []
    for time_tap in range(3):
        earlier_clip = clip_padded[time_tap:time_tap + FRAMES]
        frame_keep = (earlier_clip == clip_ids).astype(jnp.bfloat16)[:, None, None, None]
        for row_tap in range(3):
            for col_tap in range(3):
                tap_list.append(padded[time_tap:time_tap + FRAMES, row_tap:row_tap + 2 * PH, col_tap:col_tap + 2 * PW, :] * frame_keep)
    columns = jnp.concatenate(tap_list, axis=-1)
    hidden = jnp.dot(columns.reshape(-1, 27 * LC), w_in, preferred_element_type=jnp.float32) + b_in
    mean_square = lax.optimization_barrier(jnp.mean(hidden * hidden, axis=-1, keepdims=True))
    normed = hidden * lax.rsqrt(mean_square + 1e-06) * gain_in
    active = jax.nn.silu(normed).astype(jnp.bfloat16).reshape(FRAMES, 2 * PH, 2 * PW, C1)

    def one_frame(frame_act):
        upsampled = jnp.repeat(jnp.repeat(frame_act, 2, axis=0), 2, axis=1)
        upsampled = jnp.pad(upsampled, ((1, 1), (1, 1), (0, 0)))
        frame_taps = []
        for row_tap in range(3):
            for col_tap in range(3):
                frame_taps.append(upsampled[row_tap:row_tap + 4 * PH, col_tap:col_tap + 4 * PW, :])
        frame_cols = jnp.concatenate(frame_taps, axis=-1)
        result = jnp.dot(frame_cols.reshape(-1, 9 * C1), w_up, preferred_element_type=jnp.float32) + b_up
        return result.astype(jnp.bfloat16).reshape(4 * PH, 4 * PW * CO)
    return lax.map(one_frame, active)
```

```python
import math

import jax
import jax.numpy as jnp
from jax import lax
from jax.experimental import pallas as pl
from jax.experimental.pallas import tpu as pltpu
from jax.sharding import PartitionSpec as P

HEADS = 40
HD = 128
LC = 16
C1 = 384
CO = 192
PW = 16
SEQ = 8
FRM = 32
GROUPS = 5
SLOT = 32
LAT = 64
TILE_F = 4
TILES = FRM // TILE_F
TILE_Q = TILE_F * 64
BLOCK_F = 2
BLOCK_K = BLOCK_F * 128
MAX_BLOCKS = FRM // BLOCK_F
COEF = math.log2(math.e) / math.sqrt(HD)
FAR = -1e30


def pack_kernel(q_ref, k_ref, v_ref, w_ref, out_ref):
    low = lax.broadcasted_iota(jnp.int32, (8, HD), 1) < LAT
    for s in range(SEQ):
        cols = slice(s * HD, (s + 1) * HD)
        w = w_ref[cols, :]
        w2 = jnp.concatenate([w, w], axis=1)
        v = jnp.concatenate([v_ref[0, :, cols], v_ref[1, :, cols]], axis=0)
        proj = jnp.dot(v, w2, preferred_element_type=jnp.float32)
        for c in range(2):
            top = proj[c * 16 : c * 16 + 8]
            bottom = proj[c * 16 + 8 : c * 16 + 16]
            packed = jnp.where(low, top, bottom)
            k = k_ref[c, :, cols]
            q = q_ref[c, :, cols].astype(jnp.float32)
            for ab in range(2):
                tail = jnp.concatenate([packed, q[ab * 8 : ab * 8 + 8]], axis=0)
                out_ref[0, ab, c, s, 0:16, :] = k
                out_ref[0, ab, c, s, 16:32, :] = tail.astype(jnp.bfloat16)


def pack(queries, keys, values, w_head):
    span = SEQ * HD
    act = pl.BlockSpec((2, 16, span), lambda i: (0, 0, i))
    return pl.pallas_call(
        pack_kernel,
        grid=(GROUPS,),
        in_specs=[act, act, act, pl.BlockSpec((span, LAT), lambda i: (i, 0))],
        out_specs=pl.BlockSpec((1, 2, 2, SEQ, SLOT, HD), lambda i: (i, 0, 0, 0, 0, 0)),
        out_shape=jax.ShapeDtypeStruct((8, 2, 2, SEQ, SLOT, HD), jnp.bfloat16),
        compiler_params=pltpu.CompilerParams(vmem_limit_bytes=32 * 1024 * 1024),
    )(queries, keys, values, w_head)


def attend_kernel(meta_ref, own_ref, other_ref, out_ref, vt_ref, s_ref):
    lane = lax.broadcasted_iota(jnp.int32, (8, HD), 1)
    low = lane < LAT

    def spread(i, carry):
        for side, ref in enumerate((own_ref, other_ref)):
            rows = []
            for s in range(SEQ):
                packed = ref[i, s, 16:32, :].astype(jnp.float32)[0:8]
                rows.append(jnp.where(low, packed, 1.0))
                rows.append(jnp.where(low, pltpu.roll(packed, LAT, 1), 1.0))
            block = jnp.concatenate(rows, axis=0)
            vt_ref[side, i] = block.T.astype(jnp.bfloat16)
        return carry

    lax.fori_loop(0, FRM, spread, 0)

    q_frame = lax.broadcasted_iota(jnp.int32, (1, TILE_Q), 1) // 64
    row_top = lax.broadcasted_iota(jnp.int32, (8, HD), 0) < 4

    def tile(t, carry):
        first = meta_ref[2 * FRM + t]
        last = meta_ref[2 * FRM + TILES + t]
        blocks = lax.div(last - first + (BLOCK_F - 1), BLOCK_F)
        q = own_ref[pl.ds(t * TILE_F, TILE_F), :, 16:32, :].astype(jnp.float32)
        q = q[:, :, 8:16].reshape(TILE_Q, HD).astype(jnp.bfloat16)
        q_clip = jnp.zeros((1, TILE_Q), jnp.int32)
        for j in range(TILE_F):
            q_clip = jnp.where(q_frame == j, meta_ref[t * TILE_F + j], q_clip)

        def score(b, top):
            begin = first + b * BLOCK_F
            start = jnp.minimum(begin, FRM - BLOCK_F)
            for side, ref in enumerate((own_ref, other_ref)):
                k = ref[pl.ds(start, BLOCK_F), :, 0:16, :].reshape(BLOCK_K, HD)
                s = lax.dot_general(
                    k, q, (((1,), (1,)), ((), ())), preferred_element_type=jnp.float32
                )
                for j in range(BLOCK_F):
                    clip = meta_ref[side * FRM + start + j]
                    clip = jnp.where(start + j >= begin, clip, -1)
                    bias = jnp.where(q_clip == clip, 0.0, FAR)
                    part = s[j * 128 : (j + 1) * 128] + bias
                    s_ref[b, side, pl.ds(j * 128, 128), :] = part
                    top = jnp.maximum(top, jnp.max(part.reshape(16, 8, TILE_Q), axis=0))
            return top

        top = lax.fori_loop(0, blocks, score, jnp.full((8, TILE_Q), FAR, jnp.float32))
        top = jnp.max(top, axis=0, keepdims=True)

        def mix(b, total):
            start = jnp.minimum(first + b * BLOCK_F, FRM - BLOCK_F)
            for side in range(2):
                weights = jnp.exp2((s_ref[b, side] - top) * COEF).astype(jnp.bfloat16)
                for j in range(BLOCK_F):
                    total = total + jnp.dot(
                        vt_ref[side, start + j],
                        weights[j * 128 : (j + 1) * 128],
                        preferred_element_type=jnp.float32,
                    )
            return total

        total = lax.fori_loop(0, blocks, mix, jnp.zeros((HD, TILE_Q), jnp.float32))
        mixed = total[:LAT] / total[LAT : LAT + 1]
        tokens = jnp.concatenate([mixed, mixed], axis=0).T
        for j in range(TILE_Q // 16):
            a = tokens[j * 16 : j * 16 + 8]
            b = tokens[j * 16 + 8 : j * 16 + 16]
            a = jnp.where(low, a, pltpu.roll(a, 4, 0))
            b = jnp.where(low, pltpu.roll(b, 4, 0), b)
            out_ref[t, j] = jnp.where(row_top, a, b).astype(jnp.bfloat16)
        return carry

    lax.fori_loop(0, TILES, tile, 0)


def attend(meta, own, other):
    vmem = pl.BlockSpec(memory_space=pltpu.VMEM)
    return pl.pallas_call(
        attend_kernel,
        in_specs=[pl.BlockSpec(memory_space=pltpu.SMEM), vmem, vmem],
        out_specs=vmem,
        out_shape=jax.ShapeDtypeStruct((TILES, TILE_Q // 16, 8, HD), jnp.bfloat16),
        scratch_shapes=[
            pltpu.VMEM((2, FRM, HD, 128), jnp.bfloat16),
            pltpu.VMEM((MAX_BLOCKS, 2, BLOCK_K, TILE_Q), jnp.float32),
        ],
        compiler_params=pltpu.CompilerParams(vmem_limit_bytes=48 * 1024 * 1024),
    )(meta, own, other)


def passed_along(value, axis, by):
    peers = lax.axis_size(axis)
    pairs = [(i, i + by) for i in range(peers) if 0 <= i + by < peers]
    return lax.ppermute(value, axis, pairs)


def with_halo(cells, sides, width):
    for axis, dim in sides:
        count = lax.axis_size(axis)
        ends = count - 1
        head = lax.slice_in_dim(cells, 0, width, axis=dim)
        tail = lax.slice_in_dim(cells, cells.shape[dim] - width, cells.shape[dim], axis=dim)
        cells = jnp.concatenate(
            [
                lax.ppermute(tail, axis, [(i, (i + 1) % count) for i in range(ends)]),
                cells,
                lax.ppermute(head, axis, [((i + 1) % count, i) for i in range(ends)]),
            ],
            axis=dim,
        )
    return cells


def conv_layer(padded, frame_keep, out_rows, w_in, b_in, gain_in):
    frames = padded.shape[0] - 2
    lat_cols = padded.shape[2] - 2
    tap_list = []
    for time_tap in range(3):
        for row_tap in range(3):
            for col_tap in range(3):
                tap_list.append(
                    padded[
                        time_tap : time_tap + frames,
                        row_tap : row_tap + out_rows,
                        col_tap : col_tap + lat_cols,
                        :,
                    ]
                    * frame_keep[time_tap]
                )
    columns = jnp.concatenate(tap_list, axis=-1)
    hidden = (
        jnp.dot(columns.reshape(-1, columns.shape[-1]), w_in, preferred_element_type=jnp.float32)
        + b_in
    )
    mean_square = jnp.mean(hidden * hidden, axis=-1, keepdims=True)
    normed = hidden * lax.rsqrt(mean_square + 1e-06) * gain_in
    return jax.nn.silu(normed).astype(jnp.bfloat16).reshape(frames, out_rows, lat_cols, C1)


def shards(queries, keys, values, clip_ids, w_head, b_head, w_in, b_in, gain_in, w_up, b_up):
    frames = 2
    frame_position = lax.axis_index("frm")
    first_frame = frame_position * frames
    core = lax.rem(frame_position, 2)

    slots = pack(queries, keys, values, w_head).reshape(FRM * SEQ, SLOT, HD)
    own = lax.all_to_all(slots, ("frm", "seq"), 0, 0, tiled=True)
    other = lax.ppermute(own, "frm", [(i, i ^ 1) for i in range(FRM)])

    pairs = clip_ids.reshape(FRM, 2)
    own_clip = jnp.where(core == 0, pairs[:, 0], pairs[:, 1])
    other_clip = jnp.where(core == 0, pairs[:, 1], pairs[:, 0])
    below = jnp.sum(clip_ids[None, :] < own_clip[::TILE_F, None], axis=1, dtype=jnp.int32)
    upto = jnp.sum(
        clip_ids[None, :] <= own_clip[TILE_F - 1 :: TILE_F, None], axis=1, dtype=jnp.int32
    )
    meta = jnp.concatenate([own_clip, other_clip, below // 2, (upto + 1) // 2])
    mixed = attend(
        meta, own.reshape(FRM, SEQ, SLOT, HD), other.reshape(FRM, SEQ, SLOT, HD)
    ).reshape(FRM * SEQ, 4, HD)
    back = lax.all_to_all(mixed, ("frm", "seq"), 0, 0, tiled=True)
    back = back.reshape(8, 2, 2, SEQ, 4, HD)[:GROUPS].astype(jnp.float32)
    summed = jnp.sum(back, axis=(0, 3)).reshape(2, 2, 4, 2, LAT)
    latent = summed.transpose(1, 0, 3, 2, 4).reshape(frames, 16, LAT) + b_head
    latent = latent.astype(jnp.bfloat16)

    own_frames_clip = lax.dynamic_slice_in_dim(clip_ids, first_frame, frames, 0)
    patch_rows = latent.shape[1] // PW
    lat_rows = 2 * patch_rows
    lat_cols = 2 * PW
    latent_grid = (
        latent.reshape(frames, patch_rows, PW, 2, 2, LC)
        .transpose(0, 1, 3, 2, 4, 5)
        .reshape(frames, lat_rows, lat_cols, LC)
    )
    earlier = passed_along(latent_grid, "frm", 1)
    stacked = jnp.concatenate([earlier, latent_grid], axis=0)
    clip_padded = jnp.concatenate([jnp.full((2,), -1, jnp.int32), clip_ids])
    frame_keep = []
    for time_tap in range(3):
        earlier_clip = lax.dynamic_slice_in_dim(clip_padded, first_frame + time_tap, frames, 0)
        frame_keep.append(
            (earlier_clip == own_frames_clip).astype(jnp.bfloat16)[:, None, None, None]
        )
    padded = with_halo(stacked, (("seq", 1),), 1)
    padded = jnp.pad(padded, ((0, 0), (0, 0), (1, 1), (0, 0)))
    active = conv_layer(padded, frame_keep, lat_rows, w_in, b_in, gain_in)
    border = with_halo(active, (("seq", 1),), 1)
    middle = jnp.repeat(border[:, 1:-1], 2, axis=1)
    upsampled = jnp.concatenate([border[:, :1], middle, border[:, -1:]], axis=1)
    upsampled = jnp.repeat(upsampled, 2, axis=2)
    upsampled = jnp.pad(upsampled, ((0, 0), (0, 0), (1, 1), (0, 0)))
    up_rows = 2 * lat_rows
    up_cols = 2 * lat_cols
    tap_list = []
    for row_tap in range(3):
        for col_tap in range(3):
            tap_list.append(
                upsampled[:, row_tap : row_tap + up_rows, col_tap : col_tap + up_cols, :]
            )
    columns = jnp.concatenate(tap_list, axis=-1)
    result = jnp.dot(columns.reshape(-1, 9 * C1), w_up, preferred_element_type=jnp.float32) + b_up
    return result.astype(jnp.bfloat16).reshape(frames, up_rows, up_cols * CO)


def solution(mesh):
    in_specs = (
        P("frm", "seq", None),
        P("frm", "seq", None),
        P("frm", "seq", None),
        P(),
        P(),
        P(),
        P(),
        P(),
        P(),
        P(),
        P(),
    )
    out_specs = P("frm", "seq", None)
    return jax.shard_map(shards, mesh=mesh, in_specs=in_specs, out_specs=out_specs, check_vma=False)
```

```python
import math

import jax
import jax.numpy as jnp
from jax import lax
from jax.experimental import pallas as pl
from jax.experimental.pallas import tpu as pltpu
from jax.sharding import PartitionSpec as P

HEADS = 40
HD = 128
LC = 16
C1 = 384
CO = 192
PW = 16
SEQ = 8
FRM = 32
GROUPS = 5
PARTS = 3
SHARE = 6
STEP = 5
SLOT = 32
LAT = 64
FRAME_Q = SEQ * SHARE
GATHER_F = 4
GATHER_Q = GATHER_F * FRAME_Q
TILE_Q = 256
TILES = FRM * FRAME_Q // TILE_Q
TILE_SPAN = -(-TILE_Q // FRAME_Q) + 1
BLOCK_F = 9
BLOCK_K = BLOCK_F * 128
MAX_BLOCKS = -(-FRM // BLOCK_F)
COEF = math.log2(math.e) / math.sqrt(HD)
FAR = -1e30
MIB = 1024 * 1024


def pack_kernel(q_ref, k_ref, v_ref, w_ref, out_ref):
    low = lax.broadcasted_iota(jnp.int32, (8, HD), 1) < LAT
    for s in range(SEQ):
        cols = slice(s * HD, (s + 1) * HD)
        w = w_ref[cols, :]
        w2 = jnp.concatenate([w, w], axis=1)
        v = jnp.concatenate([v_ref[0, :, cols], v_ref[1, :, cols]], axis=0)
        proj = jnp.dot(v, w2, preferred_element_type=jnp.float32)
        for c in range(2):
            packed = jnp.where(low, proj[c * 8 : c * 8 + 8], proj[16 + c * 8 : 24 + c * 8])
            k = k_ref[c, :, cols]
            q = q_ref[c, :, cols].astype(jnp.float32)
            for part in range(PARTS):
                own = q if part == 0 else pltpu.roll(q, 16 - part * STEP, 0)
                tail = jnp.concatenate([packed, own[:8]], axis=0)
                out_ref[part, c, s, 0:16, :] = k
                out_ref[part, c, s, 16:32, :] = tail.astype(jnp.bfloat16)


def pack(queries, keys, values, w_head):
    span = SEQ * HD
    act = pl.BlockSpec((2, 16, span), lambda i: (0, 0, i))
    return pl.pallas_call(
        pack_kernel,
        grid=(GROUPS,),
        in_specs=[act, act, act, pl.BlockSpec((span, LAT), lambda i: (i, 0))],
        out_specs=pl.BlockSpec((PARTS, 2, SEQ, SLOT, HD), lambda i: (i, 0, 0, 0, 0)),
        out_shape=jax.ShapeDtypeStruct((FRM // 2, 2, SEQ, SLOT, HD), jnp.bfloat16),
        compiler_params=pltpu.CompilerParams(vmem_limit_bytes=32 * MIB),
    )(queries, keys, values, w_head)


def attend_kernel(
    meta_ref, own_ref, other_ref, out_ref, q_ref, vt_ref, s_ref, done_ref, pick_ref, place_ref
):
    core = meta_ref[2 * FRM + 2 * TILES]

    row = lax.broadcasted_iota(jnp.int32, (GATHER_Q, GATHER_F * 128), 0)
    col = lax.broadcasted_iota(jnp.int32, (GATHER_Q, GATHER_F * 128), 1)
    inner = lax.bitwise_and(col, 15) - 8
    hit = (row == SHARE * lax.shift_right_logical(col, 4) + inner) & (inner >= 0) & (inner < SHARE)
    pick_ref[...] = jnp.where(hit, 1.0, 0.0).astype(jnp.bfloat16)
    row = lax.broadcasted_iota(jnp.int32, (GATHER_F * 32, GATHER_F * 24), 0)
    col = lax.broadcasted_iota(jnp.int32, (GATHER_F * 32, GATHER_F * 24), 1)
    inner = lax.bitwise_and(row, 7)
    hit = (col == SHARE * lax.shift_right_logical(row, 3) + inner) & (inner < SHARE)
    place_ref[...] = jnp.where(hit, 1.0, 0.0).astype(jnp.bfloat16)

    def gather(i, carry):
        q = own_ref[pl.ds(i * GATHER_F, GATHER_F), :, 16:32, :].reshape(GATHER_F * 128, HD)
        q = jnp.dot(pick_ref[...], q, preferred_element_type=jnp.float32)
        q_ref[pl.ds(pl.multiple_of(i * GATHER_Q, GATHER_Q), GATHER_Q), :] = q.astype(jnp.bfloat16)
        return carry

    lax.fori_loop(0, FRM // GATHER_F, gather, 0)

    def spread(one, two):
        def body(i, carry):
            top = one[i, :, 16:32, :].astype(jnp.float32)[:, :8]
            bottom = two[i, :, 16:32, :].astype(jnp.float32)[:, :8]
            block = jnp.concatenate([top, bottom], axis=1).reshape(128, HD).T
            ones = jnp.ones((16, HD), jnp.float32)
            for parity in range(2):
                rows = jnp.concatenate([block[parity * LAT : (parity + 1) * LAT], ones], axis=0)
                vt_ref[parity, i] = rows.astype(jnp.bfloat16)
            return carry

        lax.fori_loop(0, FRM, body, 0)

    pl.when(core == 0)(lambda: spread(own_ref, other_ref))
    pl.when(core != 0)(lambda: spread(other_ref, own_ref))

    lane = lax.broadcasted_iota(jnp.int32, (1, TILE_Q), 1)

    def tile(t, carry):
        first = meta_ref[2 * FRM + t]
        last = meta_ref[2 * FRM + TILES + t]
        blocks = lax.div(last - first + (BLOCK_F - 1), BLOCK_F)
        rows = pl.multiple_of(t * TILE_Q, TILE_Q)
        q = q_ref[pl.ds(rows, TILE_Q), :]
        begin_f = lax.div(rows, FRAME_Q)
        q_clip = jnp.zeros((1, TILE_Q), jnp.int32)
        for j in range(TILE_SPAN):
            f = begin_f + j
            q_clip = jnp.where(
                lane + rows >= f * FRAME_Q, meta_ref[jnp.minimum(f, FRM - 1)], q_clip
            )

        def score(b, top):
            begin = first + b * BLOCK_F
            start = jnp.minimum(begin, FRM - BLOCK_F)
            for side, ref in enumerate((own_ref, other_ref)):
                k = ref[pl.ds(start, BLOCK_F), :, 0:16, :].reshape(BLOCK_K, HD)
                s = lax.dot_general(
                    k, q, (((1,), (1,)), ((), ())), preferred_element_type=jnp.float32
                )
                for j in range(BLOCK_F):
                    clip = meta_ref[side * FRM + start + j]
                    clip = jnp.where(start + j >= begin, clip, -1)
                    bias = jnp.where(q_clip == clip, 0.0, FAR)
                    part = s[j * 128 : (j + 1) * 128] + bias
                    s_ref[b, side, j * 128 : (j + 1) * 128, :] = part
                    top = jnp.maximum(top, jnp.max(part.reshape(16, 8, TILE_Q), axis=0))
            return top

        top = lax.fori_loop(0, blocks, score, jnp.full((8, TILE_Q), FAR, jnp.float32))
        top = jnp.max(top, axis=0, keepdims=True)

        def mix(b, total):
            start = jnp.minimum(first + b * BLOCK_F, FRM - BLOCK_F)
            for side in range(2):
                weights = jnp.exp2((s_ref[b, side] - top) * COEF).astype(jnp.bfloat16)
                parity = core if side == 0 else 1 - core
                vt = jnp.concatenate([vt_ref[parity, start + j] for j in range(BLOCK_F)], axis=1)
                total = total + jnp.dot(vt, weights, preferred_element_type=jnp.float32)
            return total

        total = lax.fori_loop(0, blocks, mix, jnp.zeros((LAT + 16, TILE_Q), jnp.float32))
        mixed = total[:LAT] / total[LAT : LAT + 1]
        done_ref[pl.ds(rows, TILE_Q), :] = jnp.concatenate([mixed, mixed], axis=0).T
        return carry

    lax.fori_loop(0, TILES, tile, 0)

    wide_low = lax.broadcasted_iota(jnp.int32, (FRAME_Q, HD), 1) < LAT

    def finish(i, carry):
        ratio = done_ref[pl.ds(pl.multiple_of(i * GATHER_Q, GATHER_Q), GATHER_Q), :]
        packed = []
        for j in range(0, GATHER_F, 2):
            even = ratio[j * FRAME_Q : (j + 1) * FRAME_Q]
            odd = ratio[(j + 1) * FRAME_Q : (j + 2) * FRAME_Q]
            packed.append(jnp.where(wide_low, even, odd))
        packed = jnp.concatenate(packed, axis=0).astype(jnp.bfloat16)
        placed = jnp.dot(place_ref[...], packed, preferred_element_type=jnp.float32)
        placed = placed.astype(jnp.bfloat16).reshape(GATHER_F // 2, SEQ, 8, HD)
        for j in range(GATHER_F // 2):
            for s in range(SEQ):
                for halo in range(3):
                    owner = s + 1 - halo
                    if 0 <= owner < SEQ:
                        out_ref[owner, halo, i * (GATHER_F // 2) + j] = placed[j, s]
        return carry

    lax.fori_loop(0, FRM // GATHER_F, finish, 0)


def attend(meta, own, other):
    vmem = pl.BlockSpec(memory_space=pltpu.VMEM)
    return pl.pallas_call(
        attend_kernel,
        in_specs=[pl.BlockSpec(memory_space=pltpu.SMEM), vmem, vmem],
        out_specs=vmem,
        out_shape=jax.ShapeDtypeStruct((SEQ, 3, FRM // 2, 8, HD), jnp.bfloat16),
        scratch_shapes=[
            pltpu.VMEM((FRM * FRAME_Q, HD), jnp.bfloat16),
            pltpu.VMEM((2, FRM, LAT + 16, HD), jnp.bfloat16),
            pltpu.VMEM((MAX_BLOCKS, 2, BLOCK_K, TILE_Q), jnp.float32),
            pltpu.VMEM((FRM * FRAME_Q, HD), jnp.float32),
            pltpu.VMEM((GATHER_Q, GATHER_F * 128), jnp.bfloat16),
            pltpu.VMEM((GATHER_F * 32, GATHER_F * 24), jnp.bfloat16),
        ],
        compiler_params=pltpu.CompilerParams(vmem_limit_bytes=48 * MIB),
    )(meta, own, other)


def merge_kernel(in_ref, out_ref):
    low = lax.broadcasted_iota(jnp.int32, (FRM // 2, 8, HD), 2) < LAT
    for halo in range(3):
        total = in_ref[0, halo].astype(jnp.float32)
        for head in range(1, SEQ):
            total = total + in_ref[head, halo].astype(jnp.float32)
        before = jnp.concatenate([total[:1], total[:-1]], axis=0)
        out_ref[:, 0, halo] = jnp.where(low, total, before).astype(jnp.bfloat16)
        out_ref[:, 1, halo] = total.astype(jnp.bfloat16)


def merge(parts):
    vmem = pl.BlockSpec(memory_space=pltpu.VMEM)
    return pl.pallas_call(
        merge_kernel,
        in_specs=[vmem],
        out_specs=vmem,
        out_shape=jax.ShapeDtypeStruct((FRM // 2, 2, 3, 8, HD), jnp.bfloat16),
        compiler_params=pltpu.CompilerParams(vmem_limit_bytes=32 * MIB),
    )(parts)


def conv_layer(padded, frame_keep, out_rows, w_in, b_in, gain_in):
    frames = padded.shape[0] - 2
    lat_cols = padded.shape[2] - 2
    tap_list = []
    for time_tap in range(3):
        kept = jnp.where(frame_keep[time_tap], padded[time_tap : time_tap + frames], 0)
        for row_tap in range(3):
            for col_tap in range(3):
                tap_list.append(
                    kept[:, row_tap : row_tap + out_rows, col_tap : col_tap + lat_cols, :]
                )
    columns = jnp.concatenate(tap_list, axis=-1)
    hidden = (
        jnp.dot(columns.reshape(-1, columns.shape[-1]), w_in, preferred_element_type=jnp.float32)
        + b_in
    )
    mean_square = jnp.mean(hidden * hidden, axis=-1, keepdims=True)
    normed = hidden * lax.rsqrt(mean_square + 1e-06) * gain_in
    return jax.nn.silu(normed).astype(jnp.bfloat16).reshape(frames, out_rows, lat_cols, C1)


def shards(queries, keys, values, clip_ids, w_head, b_head, w_in, b_in, gain_in, w_up, b_up):
    frames = 2
    frame_position = lax.axis_index("frm")
    row_position = lax.axis_index("seq")
    first_frame = frame_position * frames
    core = lax.rem(frame_position, 2)

    slots = pack(queries, keys, values, w_head).reshape(FRM * SEQ, SLOT, HD)
    own = lax.all_to_all(slots, ("frm", "seq"), 0, 0, tiled=True)
    other = lax.ppermute(own, "frm", [(i, i ^ 1) for i in range(FRM)])

    pairs = clip_ids.reshape(FRM, 2)
    own_clip = jnp.where(core == 0, pairs[:, 0], pairs[:, 1])
    other_clip = jnp.where(core == 0, pairs[:, 1], pairs[:, 0])
    head_clip = own_clip[jnp.array([t * TILE_Q // FRAME_Q for t in range(TILES)])]
    tail_clip = own_clip[jnp.array([((t + 1) * TILE_Q - 1) // FRAME_Q for t in range(TILES)])]
    below = jnp.sum(clip_ids[None, :] < head_clip[:, None], axis=1, dtype=jnp.int32)
    upto = jnp.sum(clip_ids[None, :] <= tail_clip[:, None], axis=1, dtype=jnp.int32)
    meta = jnp.concatenate([own_clip, other_clip, below // 2, (upto + 1) // 2, core[None]])
    mixed = attend(
        meta, own.reshape(FRM, SEQ, SLOT, HD), other.reshape(FRM, SEQ, SLOT, HD)
    ).reshape(SEQ, -1, HD)
    by_row = lax.all_to_all(mixed, "seq", 0, 0, tiled=True)
    merged = merge(by_row.reshape(SEQ, 3, FRM // 2, 8, HD)).reshape(FRM, 24, HD)
    back = lax.all_to_all(merged, "frm", 0, 0, tiled=True)

    back = back[: 2 * PARTS * GROUPS].reshape(GROUPS, PARTS, 2, 3, 8, 2, LAT)
    summed = jnp.sum(back.astype(jnp.float32), axis=0)
    summed = jnp.concatenate([summed[0, :, :, :6], summed[1, :, :, 1:6], summed[2, :, :, 1:6]], axis=2)
    halves = (summed[:, :, :, 0], summed[:, :, :, 1])
    stacked = jnp.concatenate(
        [jnp.where(core == 0, halves[1], halves[0]), jnp.where(core == 0, halves[0], halves[1])],
        axis=0,
    )
    latent = (stacked + b_head).astype(jnp.bfloat16)
    inside = row_position + jnp.arange(3) - 1
    inside = (inside >= 0) & (inside < SEQ)
    latent = jnp.where(inside[None, :, None, None], latent, 0)
    lat_cols = 2 * PW
    grid = (
        latent.reshape(2 * frames, 3, PW, 2, 2, LC)
        .transpose(0, 1, 3, 2, 4, 5)
        .reshape(2 * frames, 6, lat_cols, LC)
    )
    own_frames_clip = lax.dynamic_slice_in_dim(clip_ids, first_frame, frames, 0)
    clip_padded = jnp.concatenate([jnp.full((2,), -1, jnp.int32), clip_ids])
    frame_keep = []
    for time_tap in range(3):
        earlier_clip = lax.dynamic_slice_in_dim(clip_padded, first_frame + time_tap, frames, 0)
        frame_keep.append((earlier_clip == own_frames_clip)[:, None, None, None])
    padded = jnp.pad(grid, ((0, 0), (0, 0), (1, 1), (0, 0)))
    border = conv_layer(padded, frame_keep, 4, w_in, b_in, gain_in)
    seen = 2 * row_position + jnp.arange(4) - 1
    seen = (seen >= 0) & (seen < 2 * SEQ)
    border = jnp.where(seen[None, :, None, None], border, 0)
    middle = jnp.repeat(border[:, 1:-1], 2, axis=1)
    upsampled = jnp.concatenate([border[:, :1], middle, border[:, -1:]], axis=1)
    upsampled = jnp.repeat(upsampled, 2, axis=2)
    upsampled = jnp.pad(upsampled, ((0, 0), (0, 0), (1, 1), (0, 0)))
    up_rows = 4
    up_cols = 2 * lat_cols
    tap_list = []
    for row_tap in range(3):
        for col_tap in range(3):
            tap_list.append(
                upsampled[:, row_tap : row_tap + up_rows, col_tap : col_tap + up_cols, :]
            )
    columns = jnp.concatenate(tap_list, axis=-1)
    result = jnp.dot(columns.reshape(-1, 9 * C1), w_up, preferred_element_type=jnp.float32) + b_up
    return result.astype(jnp.bfloat16).reshape(frames, up_rows, up_cols * CO)


def solution(mesh):
    in_specs = (
        P("frm", "seq", None),
        P("frm", "seq", None),
        P("frm", "seq", None),
        P(),
        P(),
        P(),
        P(),
        P(),
        P(),
        P(),
        P(),
    )
    out_specs = P("frm", "seq", None)
    return jax.shard_map(shards, mesh=mesh, in_specs=in_specs, out_specs=out_specs, check_vma=False)
```

```python
import math

import jax
import jax.numpy as jnp
import numpy as np
from jax import lax
from jax.experimental import pallas as pl
from jax.experimental.pallas import tpu as pltpu
from jax.sharding import PartitionSpec as P

HEADS = 40
HD = 128
LC = 16
C1 = 384
CO = 192
SEQ = 8
FRM = 32
GROUPS = 5
PARTS = 3
SHARE = 6
STEP = 5
SLOT = 32
LAT = 64
SPAN = SEQ * HD
FRAME_Q = SEQ * SHARE
GATHER_F = 4
GATHER_Q = GATHER_F * FRAME_Q
TILE_Q = 256
TILES = FRM * FRAME_Q // TILE_Q
TILE_SPAN = -(-TILE_Q // FRAME_Q) + 1
BLOCK_F = 9
BLOCK_K = BLOCK_F * 128
MAX_BLOCKS = -(-FRM // BLOCK_F)
COEF = math.log2(math.e) / math.sqrt(HD)
FAR = -1e30
MIB = 1024 * 1024
NT = (((1,), (1,)), ((), ()))


def pack_kernel(q_hbm, k_hbm, v_hbm, w_hbm, out_ref, q_ref, k_ref, v_ref, w_ref, sems):
    copies = []
    for g in range(GROUPS):
        cols = slice(g * SPAN, (g + 1) * SPAN)
        group = []
        for i, (src, dst) in enumerate(
            ((v_hbm, v_ref), (k_hbm, k_ref), (q_hbm, q_ref), (w_hbm, w_ref))
        ):
            where = (slice(None), cols) if i == 3 else (slice(None), slice(None), cols)
            copy = pltpu.make_async_copy(src.at[where], dst.at[where], sems.at[g, i])
            copy.start()
            group.append(copy)
        copies.append(group)
    low = lax.broadcasted_iota(jnp.int32, (8, HD), 1) < LAT
    for g in range(GROUPS):
        for copy in copies[g]:
            copy.wait()
        for s in range(SEQ):
            cols = slice(g * SPAN + s * HD, g * SPAN + (s + 1) * HD)
            w = w_ref[:, cols]
            w2 = jnp.concatenate([w, w], axis=0)
            v = jnp.concatenate([v_ref[0, :, cols], v_ref[1, :, cols]], axis=0)
            proj = lax.dot_general(v, w2, NT, preferred_element_type=jnp.float32)
            keys = [k_ref[p, :, cols].astype(jnp.float32) for p in range(2)]
            for c in range(2):
                half = slice(c * 8, c * 8 + 8)
                k = jnp.concatenate([keys[0][half], keys[1][half]], axis=0).astype(jnp.bfloat16)
                packed = jnp.where(low, proj[c * 8 : c * 8 + 8], proj[16 + c * 8 : 24 + c * 8])
                q = q_ref[c, :, cols].astype(jnp.float32)
                for part in range(PARTS):
                    own = q if part == 0 else pltpu.roll(q, 16 - part * STEP, 0)
                    tail = jnp.concatenate([packed, own[:8]], axis=0)
                    out_ref[g * PARTS + part, c, s, 0:16, :] = k
                    out_ref[g * PARTS + part, c, s, 16:32, :] = tail.astype(jnp.bfloat16)


def pack(queries, keys, values, w_head):
    hbm = pl.BlockSpec(memory_space=pltpu.HBM)
    act = pltpu.VMEM((2, 16, HEADS * HD), jnp.bfloat16)
    return pl.pallas_call(
        pack_kernel,
        in_specs=[hbm, hbm, hbm, hbm],
        out_specs=pl.BlockSpec(memory_space=pltpu.VMEM),
        out_shape=pltpu.VMEM((FRM // 2, 2, SEQ, SLOT, HD), jnp.bfloat16),
        scratch_shapes=[
            act,
            act,
            act,
            pltpu.VMEM((LAT, HEADS * HD), jnp.bfloat16),
            pltpu.SemaphoreType.DMA((GROUPS, 4)),
        ],
        compiler_params=pltpu.CompilerParams(vmem_limit_bytes=12 * MIB),
    )(*(pltpu.with_memory_space_constraint(x, pltpu.HBM) for x in (queries, keys, values, w_head.T)))


def prepare_kernel(in_ref, kv_ref, q_ref, pick_ref):
    row = lax.broadcasted_iota(jnp.int32, (2 * FRAME_Q, 256), 0)
    col = lax.broadcasted_iota(jnp.int32, (2 * FRAME_Q, 256), 1)
    inner = lax.bitwise_and(col, 15) - 8
    hit = (row == SHARE * lax.shift_right_logical(col, 4) + inner) & (inner >= 0) & (inner < SHARE)
    pick_ref[...] = jnp.where(hit, 1.0, 0.0).astype(jnp.bfloat16)

    def body(i, carry):
        for j in range(2):
            f = 2 * i + j
            kv_ref[f, 0:128, :] = in_ref[f, :, 0:16, :].reshape(128, HD)
            packed = in_ref[f, :, 16:32, :].astype(jnp.float32)[:, :8]
            rolled = pltpu.roll(packed.reshape(SEQ * 8, HD), LAT, 1).reshape(SEQ, 8, HD)
            block = jnp.concatenate([packed, rolled], axis=1).reshape(128, HD).T
            kv_ref[f, 128:192, :] = block[:LAT].astype(jnp.bfloat16)
        q = in_ref[pl.ds(2 * i, 2), :, 16:32, :].reshape(256, HD)
        q = jnp.dot(pick_ref[...], q, preferred_element_type=jnp.float32)
        rows = pl.multiple_of(i * 2 * FRAME_Q, 2 * FRAME_Q)
        q_ref[pl.ds(rows, 2 * FRAME_Q), :] = q.astype(jnp.bfloat16)
        return carry

    lax.fori_loop(0, FRM // 2, body, 0)


def prepare(own):
    vmem = pl.BlockSpec(memory_space=pltpu.VMEM)
    return pl.pallas_call(
        prepare_kernel,
        in_specs=[vmem],
        out_specs=[vmem, vmem],
        out_shape=[
            pltpu.VMEM((FRM, 128 + LAT, HD), jnp.bfloat16),
            pltpu.VMEM((FRM * FRAME_Q, HD), jnp.bfloat16),
        ],
        scratch_shapes=[pltpu.VMEM((2 * FRAME_Q, 256), jnp.bfloat16)],
        compiler_params=pltpu.CompilerParams(vmem_limit_bytes=12 * MIB),
    )(own)


def attend_kernel(meta_ref, q_ref, own_ref, other_ref, out_ref, s_ref, done_ref, place_ref):
    core = meta_ref[3, 0]
    row = lax.broadcasted_iota(jnp.int32, (GATHER_F * 32, GATHER_F * 24), 0)
    col = lax.broadcasted_iota(jnp.int32, (GATHER_F * 32, GATHER_F * 24), 1)
    inner = lax.bitwise_and(row, 7)
    hit = (col == SHARE * lax.shift_right_logical(row, 3) + inner) & (inner < SHARE)
    place_ref[...] = jnp.where(hit, 1.0, 0.0).astype(jnp.bfloat16)
    ones = jnp.ones((16, BLOCK_K), jnp.bfloat16)
    lane = lax.broadcasted_iota(jnp.int32, (8, TILE_Q), 1)

    def tile(t, carry):
        rows = pl.multiple_of(t * TILE_Q, TILE_Q)
        q = q_ref[pl.ds(rows, TILE_Q), :]
        begin_f = lax.div(rows, FRAME_Q)
        end_f = lax.div(rows + (TILE_Q - 1), FRAME_Q)
        first = lax.shift_right_logical(meta_ref[1, 2 * begin_f + core], 1)
        last = lax.shift_right_logical(meta_ref[2, 2 * end_f + core] + 1, 1)
        blocks = lax.div(last - first + (BLOCK_F - 1), BLOCK_F)
        q_clip = jnp.zeros((8, TILE_Q), jnp.int32)
        for j in range(TILE_SPAN):
            f = begin_f + j
            clip = meta_ref[0, jnp.minimum(2 * f + core, 2 * FRM - 1)]
            q_clip = jnp.where(lane + rows >= f * FRAME_Q, clip, q_clip)

        def score(b, top):
            begin = first + b * BLOCK_F
            start = jnp.minimum(begin, FRM - BLOCK_F)
            biases = []
            for j in range(BLOCK_F):
                pair = []
                for p in range(2):
                    clip = meta_ref[0, 2 * (start + j) + p]
                    clip = jnp.where(start + j >= begin, clip, -1)
                    pair.append(jnp.where(q_clip == clip, 0.0, FAR))
                biases.append(jnp.concatenate(pair, axis=0)[None])
            for side, ref in enumerate((own_ref, other_ref)):
                k = ref[pl.ds(start, BLOCK_F), 0:128, :].reshape(BLOCK_K, HD)
                s = lax.dot_general(k, q, NT, preferred_element_type=jnp.float32)
                for j in range(BLOCK_F):
                    part = s[j * 128 : (j + 1) * 128].reshape(SEQ, 16, TILE_Q) + biases[j]
                    s_ref[b, side, j * 128 : (j + 1) * 128, :] = part.reshape(128, TILE_Q)
                    top = jnp.maximum(top, jnp.max(part.reshape(16, 8, TILE_Q), axis=0))
            return top

        top = lax.fori_loop(0, blocks, score, jnp.full((8, TILE_Q), FAR, jnp.float32))
        top = jnp.max(top, axis=0, keepdims=True)

        def mix(b, total):
            start = jnp.minimum(first + b * BLOCK_F, FRM - BLOCK_F)
            for side, ref in enumerate((own_ref, other_ref)):
                weights = jnp.exp2((s_ref[b, side] - top) * COEF).astype(jnp.bfloat16)
                vt = [ref[start + j, 128 : 128 + LAT, :] for j in range(BLOCK_F)]
                vt = jnp.concatenate([jnp.concatenate(vt, axis=1), ones], axis=0)
                total = total + jnp.dot(vt, weights, preferred_element_type=jnp.float32)
            return total

        total = lax.fori_loop(0, blocks, mix, jnp.zeros((LAT + 16, TILE_Q), jnp.float32))
        mixed = total[:LAT] / total[LAT : LAT + 1]
        done_ref[pl.ds(rows, TILE_Q), :] = jnp.concatenate([mixed, mixed], axis=0).T
        return carry

    lax.fori_loop(0, TILES, tile, 0)

    wide_low = lax.broadcasted_iota(jnp.int32, (FRAME_Q, HD), 1) < LAT

    def finish(i, carry):
        ratio = done_ref[pl.ds(pl.multiple_of(i * GATHER_Q, GATHER_Q), GATHER_Q), :]
        packed = []
        for j in range(0, GATHER_F, 2):
            even = ratio[j * FRAME_Q : (j + 1) * FRAME_Q]
            odd = ratio[(j + 1) * FRAME_Q : (j + 2) * FRAME_Q]
            packed.append(jnp.where(wide_low, even, odd))
        packed = jnp.concatenate(packed, axis=0).astype(jnp.bfloat16)
        placed = jnp.dot(place_ref[...], packed, preferred_element_type=jnp.float32)
        placed = placed.astype(jnp.bfloat16).reshape(GATHER_F // 2, SEQ, 8, HD)
        for j in range(GATHER_F // 2):
            for s in range(SEQ):
                for halo in range(3):
                    owner = s + 1 - halo
                    if 0 <= owner < SEQ:
                        out_ref[owner, halo, i * (GATHER_F // 2) + j] = placed[j, s]
        return carry

    lax.fori_loop(0, FRM // GATHER_F, finish, 0)


def attend(meta, q, own, other):
    vmem = pl.BlockSpec(memory_space=pltpu.VMEM)
    return pl.pallas_call(
        attend_kernel,
        in_specs=[pl.BlockSpec(memory_space=pltpu.SMEM), vmem, vmem, vmem],
        out_specs=vmem,
        out_shape=pltpu.VMEM((SEQ, 3, FRM // 2, 8, HD), jnp.bfloat16),
        scratch_shapes=[
            pltpu.VMEM((MAX_BLOCKS, 2, BLOCK_K, TILE_Q), jnp.float32),
            pltpu.VMEM((FRM * FRAME_Q, HD), jnp.float32),
            pltpu.VMEM((GATHER_F * 32, GATHER_F * 24), jnp.bfloat16),
        ],
        compiler_params=pltpu.CompilerParams(vmem_limit_bytes=24 * MIB),
    )(meta, q, own, other)


def merge_kernel(in_ref, out_ref):
    low = lax.broadcasted_iota(jnp.int32, (FRM // 2, 8, HD), 2) < LAT
    for halo in range(3):
        total = in_ref[0, halo].astype(jnp.float32)
        for head in range(1, SEQ):
            total = total + in_ref[head, halo].astype(jnp.float32)
        before = jnp.concatenate([total[:1], total[:-1]], axis=0)
        out_ref[:, 0, halo] = jnp.where(low, total, before).astype(jnp.bfloat16)
        out_ref[:, 1, halo] = total.astype(jnp.bfloat16)


def merge(parts):
    vmem = pl.BlockSpec(memory_space=pltpu.VMEM)
    return pl.pallas_call(
        merge_kernel,
        in_specs=[vmem],
        out_specs=vmem,
        out_shape=pltpu.VMEM((FRM // 2, 2, 3, 8, HD), jnp.bfloat16),
        compiler_params=pltpu.CompilerParams(vmem_limit_bytes=12 * MIB),
    )(parts)


def assembly():
    out = np.zeros((3, 2, 3, 16, PARTS, 2, 3, 8), np.float32)
    for near in range(3):
        for token in range(16):
            source = token + near - 1
            if 0 <= source < 16:
                part = min(max(source - 1, 0) // STEP, PARTS - 1)
                for c in range(2):
                    for h in range(3):
                        out[near, c, h, token, part, c, h, source - part * STEP] = 1
    return out.reshape(3 * 96, 144)


def spreading():
    out = np.zeros((3, 2, 2, 2, LC, 2, 2, 2, 128), np.float32)
    for parity in range(2):
        for tap in range(3):
            column = parity + tap - 1
            near, b = 1 + column // 2, column % 2
            for pair in range(2):
                for a in range(2):
                    for ch in range(LC):
                        out[near, pair, a, b, ch, pair, a, parity, tap * LC + ch] = 1
    return out.reshape(3 * HD, 8 * 128)


def reordering():
    out = np.zeros((3, 16, 2, 2, 4, 2, 2, 4, 16), np.float32)
    for tap in range(3):
        for row in range(4):
            source = (row + tap + 1) // 2
            for frame in range(2):
                for parity in range(2):
                    for column in range(16):
                        out[tap, column, parity, frame, row, frame, parity, source, column] = 1
    return out.reshape(3, 256, 256)


def decode_kernel(
    clip_ref, place_ref, in_ref, gather_ref, spread_ref, order_ref, b_head_ref, w_in_ref, b_in_ref,
    gain_ref, w_up_ref, b_up_ref, out_ref,
):
    first_frame = 2 * place_ref[0]
    core = lax.rem(place_ref[0], 2)
    no_above = place_ref[1] == 0
    no_below = place_ref[1] == SEQ - 1
    total = in_ref[0].astype(jnp.float32)
    for g in range(1, GROUPS):
        total = total + in_ref[g].astype(jnp.float32)
    total = total + b_head_ref[...]
    total = total.reshape(144, HD)
    total = jnp.where(core == 0, pltpu.roll(total, LAT, 1), total)
    row = lax.broadcasted_iota(jnp.int32, (144, HD), 0)
    patch = lax.rem(lax.shift_right_logical(row, 3), 3)
    outside = ((patch == 0) & no_above) | ((patch == 2) & no_below)
    tokens = jnp.where(outside, 0.0, total).astype(jnp.bfloat16)
    tokens = jnp.dot(gather_ref[...], tokens, preferred_element_type=jnp.float32)
    tokens = tokens.astype(jnp.bfloat16)
    near = jnp.concatenate([tokens[i * 96 : (i + 1) * 96] for i in range(3)], axis=1)
    cells = jnp.dot(near, spread_ref[...], preferred_element_type=jnp.float32).astype(jnp.bfloat16)

    hidden = jnp.zeros((256, C1), jnp.float32)
    for time_tap in (2, 1, 0):
        part = jnp.zeros((256, C1), jnp.float32)
        for row_tap in range(3):
            pieces = []
            for f in range(2):
                pair, c = divmod(f + time_tap, 2)
                for parity in range(2):
                    for r in range(4):
                        h, a = divmod(r + row_tap, 2)
                        e = (pair * 2 + a) * 2 + parity
                        rows = slice((c * 3 + h) * 16, (c * 3 + h + 1) * 16)
                        pieces.append(cells[rows, e * 128 : e * 128 + 3 * LC])
            columns = jnp.concatenate(pieces, axis=0)
            tap = (time_tap * 3 + row_tap) * 3 * LC
            part = part + jnp.dot(
                columns, w_in_ref[tap : tap + 3 * LC, :], preferred_element_type=jnp.float32
            )
        if time_tap == 2:
            hidden = part + b_in_ref[...]
        else:
            kept = []
            for f in range(2):
                earlier = first_frame + (f + time_tap - 2)
                same = clip_ref[jnp.maximum(earlier, 0)] == clip_ref[first_frame + f]
                keep = (earlier >= 0) & same
                kept.append(jnp.where(keep, part[f * 128 : (f + 1) * 128], 0.0))
            hidden = hidden + jnp.concatenate(kept, axis=0)
    mean_square = jnp.mean(hidden * hidden, axis=-1, keepdims=True)
    normed = hidden * lax.rsqrt(mean_square + 1e-06) * gain_ref[...]
    active = normed / (1.0 + jnp.exp(-normed))
    row = lax.broadcasted_iota(jnp.int32, (256, C1), 0)
    grid_row = lax.bitwise_and(lax.shift_right_logical(row, 4), 3)
    outside = ((grid_row == 0) & no_above) | ((grid_row == 3) & no_below)
    active = jnp.where(outside, 0.0, active).astype(jnp.bfloat16)

    taps = [jnp.zeros((256, CO), jnp.float32) for _ in range(3)]
    for row_tap in range(3):
        placed = jnp.dot(order_ref[row_tap], active, preferred_element_type=jnp.float32)
        placed = placed.astype(jnp.bfloat16)
        for col_tap in range(3):
            tap = (row_tap * 3 + col_tap) * C1
            taps[col_tap] = taps[col_tap] + lax.dot_general(
                placed, w_up_ref[:, tap : tap + C1], NT, preferred_element_type=jnp.float32
            )
    edge = jnp.zeros((8, CO), jnp.float32)
    before = jnp.concatenate([edge, taps[0][:-8]], axis=0)
    after = jnp.concatenate([taps[2][8:], edge], axis=0)
    even = before + taps[1] + taps[2] + b_up_ref[...]
    odd = taps[0] + taps[1] + after + b_up_ref[...]
    both = jnp.concatenate([even, odd], axis=1).astype(jnp.bfloat16).astype(jnp.float32)
    for column in range(32):
        piece = both[column * 8 : column * 8 + 8]
        lanes = slice(column * 2 * CO, (column + 1) * 2 * CO)
        out_ref[0, :, lanes] = piece[:4].astype(jnp.bfloat16)
        out_ref[1, :, lanes] = piece[4:].astype(jnp.bfloat16)


def decode(clip_ids, place, back, b_head, w_in, b_in, gain_in, w_up, b_up):
    vmem = pl.BlockSpec(memory_space=pltpu.VMEM)
    constants = [jnp.asarray(x, jnp.bfloat16) for x in (assembly(), spreading(), reordering())]
    return pl.pallas_call(
        decode_kernel,
        in_specs=[pl.BlockSpec(memory_space=pltpu.SMEM)] * 2 + [vmem] * 10,
        out_specs=vmem,
        out_shape=jax.ShapeDtypeStruct((2, 4, 64 * CO), jnp.bfloat16),
        compiler_params=pltpu.CompilerParams(vmem_limit_bytes=12 * MIB),
    )(
        clip_ids,
        place,
        back,
        *constants,
        jnp.concatenate([b_head, b_head])[None],
        w_in,
        b_in[None],
        gain_in[None],
        w_up.T,
        b_up[None],
    )


def shards(queries, keys, values, clip_ids, w_head, b_head, w_in, b_in, gain_in, w_up, b_up):
    frame_position = lax.axis_index("frm")
    row_position = lax.axis_index("seq")
    core = lax.rem(frame_position, 2)

    slots = pack(queries, keys, values, w_head).reshape(FRM * SEQ, SLOT, HD)
    own = lax.all_to_all(slots, ("frm", "seq"), 0, 0, tiled=True)
    own_kv, own_q = prepare(own.reshape(FRM, SEQ, SLOT, HD))
    other_kv = lax.ppermute(own_kv, "frm", [(i, i ^ 1) for i in range(FRM)])

    below = jnp.sum(clip_ids[None, :] < clip_ids[:, None], axis=1, dtype=jnp.int32)
    upto = jnp.sum(clip_ids[None, :] <= clip_ids[:, None], axis=1, dtype=jnp.int32)
    kind = lax.broadcasted_iota(jnp.int32, (4, 2 * FRM), 0)
    meta = jnp.where(kind == 0, clip_ids, jnp.where(kind == 1, below, jnp.where(kind == 2, upto, core)))
    mixed = attend(meta, own_q, own_kv, other_kv).reshape(SEQ, -1, HD)
    by_row = lax.all_to_all(mixed, "seq", 0, 0, tiled=True)
    merged = merge(by_row.reshape(SEQ, 3, FRM // 2, 8, HD)).reshape(FRM, 24, HD)
    back = lax.all_to_all(merged, "frm", 0, 0, tiled=True)

    back = back[: 2 * PARTS * GROUPS].reshape(GROUPS, 2 * PARTS, 24, HD)
    place = jnp.where(jnp.arange(2) == 0, frame_position, row_position)
    return decode(clip_ids, place, back, b_head, w_in, b_in, gain_in, w_up, b_up)


def solution(mesh):
    in_specs = (
        P("frm", "seq", None),
        P("frm", "seq", None),
        P("frm", "seq", None),
        P(),
        P(),
        P(),
        P(),
        P(),
        P(),
        P(),
        P(),
    )
    out_specs = P("frm", "seq", None)
    return jax.shard_map(shards, mesh=mesh, in_specs=in_specs, out_specs=out_specs, check_vma=False)
```

```python
import math

import jax
import jax.numpy as jnp
import numpy as np
from jax import lax
from jax.experimental import pallas as pl
from jax.experimental.pallas import tpu as pltpu
from jax.sharding import PartitionSpec as P

HEADS = 40
HD = 128
LC = 16
C1 = 384
CO = 192
SEQ = 8
FRM = 32
GROUPS = 5
PARTS = 3
SHARE = 6
STEP = 5
SLOT = 32
LAT = 64
SPAN = SEQ * HD
FRAME_Q = SEQ * SHARE
GATHER_F = 8
GATHER_R = GATHER_F // 2 * SHARE
TILE_Q = 256
TILES = FRM * FRAME_Q // TILE_Q
TILE_SPAN = -(-TILE_Q // FRAME_Q) + 1
BLOCK_F = 17
GROUP = 2
BLOCK_K = BLOCK_F * 128
MAX_BLOCKS = -(-FRM // BLOCK_F)
COEF = math.log2(math.e) / math.sqrt(HD)
FAR = -1e30
MIB = 1024 * 1024
NT = (((1,), (1,)), ((), ()))


def pack_kernel(q_hbm, k_hbm, v_hbm, w_hbm, out_ref, q_ref, k_ref, v_ref, w_ref, sems):
    copies = []
    for g in range(GROUPS):
        cols = slice(g * SPAN, (g + 1) * SPAN)
        group = []
        for i, (src, dst) in enumerate(
            ((v_hbm, v_ref), (k_hbm, k_ref), (q_hbm, q_ref), (w_hbm, w_ref))
        ):
            where = (slice(None), cols) if i == 3 else (slice(None), slice(None), cols)
            copy = pltpu.make_async_copy(src.at[where], dst.at[where], sems.at[g, i])
            copy.start()
            group.append(copy)
        copies.append(group)
    low = lax.broadcasted_iota(jnp.int32, (8, HD), 1) < LAT
    for g in range(GROUPS):
        for copy in copies[g]:
            copy.wait()
        for s in range(SEQ):
            cols = slice(g * SPAN + s * HD, g * SPAN + (s + 1) * HD)
            w = w_ref[:, cols]
            w2 = jnp.concatenate([w, w], axis=0)
            v = jnp.concatenate([v_ref[0, :, cols], v_ref[1, :, cols]], axis=0)
            proj = lax.dot_general(v, w2, NT, preferred_element_type=jnp.float32)
            keys = [k_ref[p, :, cols].astype(jnp.float32) for p in range(2)]
            for c in range(2):
                half = slice(c * 8, c * 8 + 8)
                k = jnp.concatenate([keys[0][half], keys[1][half]], axis=0).astype(jnp.bfloat16)
                packed = jnp.where(low, proj[c * 8 : c * 8 + 8], proj[16 + c * 8 : 24 + c * 8])
                q = q_ref[c, :, cols].astype(jnp.float32)
                for part in range(PARTS):
                    own = q if part == 0 else pltpu.roll(q, 16 - part * STEP, 0)
                    tail = jnp.concatenate([packed, own[:8]], axis=0)
                    out_ref[g * PARTS + part, c, s, 0:16, :] = k
                    out_ref[g * PARTS + part, c, s, 16:32, :] = tail.astype(jnp.bfloat16)


def pack(queries, keys, values, w_head):
    hbm = pl.BlockSpec(memory_space=pltpu.HBM)
    act = pltpu.VMEM((2, 16, HEADS * HD), jnp.bfloat16)
    return pl.pallas_call(
        pack_kernel,
        in_specs=[hbm, hbm, hbm, hbm],
        out_specs=pl.BlockSpec(memory_space=pltpu.VMEM),
        out_shape=pltpu.VMEM((FRM // 2, 2, SEQ, SLOT, HD), jnp.bfloat16),
        scratch_shapes=[
            act,
            act,
            act,
            pltpu.VMEM((LAT, HEADS * HD), jnp.bfloat16),
            pltpu.SemaphoreType.DMA((GROUPS, 4)),
        ],
        compiler_params=pltpu.CompilerParams(vmem_limit_bytes=12 * MIB),
    )(*(pltpu.with_memory_space_constraint(x, pltpu.HBM) for x in (queries, keys, values, w_head.T)))


def prepare_kernel(in_ref, kv_ref, q_ref, pick_ref):
    row = lax.broadcasted_iota(jnp.int32, (2 * FRAME_Q, 256), 0)
    col = lax.broadcasted_iota(jnp.int32, (2 * FRAME_Q, 256), 1)
    inner = lax.bitwise_and(col, 15) - 8
    hit = (row == SHARE * lax.shift_right_logical(col, 4) + inner) & (inner >= 0) & (inner < SHARE)
    pick_ref[...] = jnp.where(hit, 1.0, 0.0).astype(jnp.bfloat16)

    def body(i, carry):
        for j in range(2):
            f = 2 * i + j
            kv_ref[f, 0:128, :] = in_ref[f, :, 0:16, :].reshape(128, HD)
            packed = in_ref[f, :, 16:32, :].astype(jnp.float32)[:, :8]
            rolled = pltpu.roll(packed.reshape(SEQ * 8, HD), LAT, 1).reshape(SEQ, 8, HD)
            block = jnp.concatenate([packed, rolled], axis=1).reshape(128, HD).T
            kv_ref[f, 128:192, :] = block[:LAT].astype(jnp.bfloat16)
        q = in_ref[pl.ds(2 * i, 2), :, 16:32, :].reshape(256, HD)
        q = jnp.dot(pick_ref[...], q, preferred_element_type=jnp.float32)
        rows = pl.multiple_of(i * 2 * FRAME_Q, 2 * FRAME_Q)
        q_ref[pl.ds(rows, 2 * FRAME_Q), :] = q.astype(jnp.bfloat16)
        return carry

    lax.fori_loop(0, FRM // 2, body, 0, unroll=16)


def prepare(own):
    vmem = pl.BlockSpec(memory_space=pltpu.VMEM)
    return pl.pallas_call(
        prepare_kernel,
        in_specs=[vmem],
        out_specs=[vmem, vmem],
        out_shape=[
            pltpu.VMEM((FRM, 128 + LAT, HD), jnp.bfloat16),
            pltpu.VMEM((FRM * FRAME_Q, HD), jnp.bfloat16),
        ],
        scratch_shapes=[pltpu.VMEM((2 * FRAME_Q, 256), jnp.bfloat16)],
        compiler_params=pltpu.CompilerParams(vmem_limit_bytes=12 * MIB),
    )(own)


def attend_kernel(meta_ref, q_ref, own_ref, other_ref, out_ref, s_ref, done_ref, place_ref):
    core = meta_ref[3, 0]
    share = lax.broadcasted_iota(jnp.int32, (SEQ * GATHER_R, 1), 0)
    source = jnp.zeros_like(share)
    for size, unit, stop in ((GATHER_R, SHARE, SEQ), (SHARE, FRAME_Q, GATHER_F // 2)):
        count = jnp.zeros_like(share)
        for i in range(1, stop):
            count = count + jnp.where(share >= size * i, 1, 0)
        share = share - count * size
        source = source + count * unit
    col = lax.broadcasted_iota(jnp.int32, (SEQ * GATHER_R, SEQ * GATHER_R), 1)
    place_ref[...] = jnp.where(col == source + share, 1.0, 0.0).astype(jnp.bfloat16)
    ones = jnp.ones((16, BLOCK_K), jnp.bfloat16)
    lane = lax.broadcasted_iota(jnp.int32, (8, TILE_Q), 1)

    def setup(t):
        rows = pl.multiple_of(t * TILE_Q, TILE_Q)
        q = q_ref[pl.ds(rows, TILE_Q), :]
        begin_f = lax.div(rows, FRAME_Q)
        end_f = lax.div(rows + (TILE_Q - 1), FRAME_Q)
        first = lax.shift_right_logical(meta_ref[1, 2 * begin_f + core], 1)
        last = lax.shift_right_logical(meta_ref[2, 2 * end_f + core] + 1, 1)
        blocks = lax.div(last - first + (BLOCK_F - 1), BLOCK_F)
        q_clip = jnp.zeros((8, TILE_Q), jnp.int32)
        for j in range(TILE_SPAN):
            f = begin_f + j
            clip = meta_ref[0, jnp.minimum(2 * f + core, 2 * FRM - 1)]
            q_clip = jnp.where(lane + rows >= f * FRAME_Q, clip, q_clip)
        return rows, q, q_clip, first, blocks

    def score(b, q, q_clip, first, buffer, top):
        begin = first + b * BLOCK_F
        start = jnp.minimum(begin, FRM - BLOCK_F)
        biases = []
        for j in range(BLOCK_F):
            pair = []
            for p in range(2):
                clip = meta_ref[0, 2 * (start + j) + p]
                clip = jnp.where(start + j >= begin, clip, -1)
                pair.append(jnp.where(q_clip == clip, 0.0, FAR))
            biases.append(jnp.concatenate(pair, axis=0)[None])
        for side, ref in enumerate((own_ref, other_ref)):
            k = ref[pl.ds(start, BLOCK_F), 0:128, :].reshape(BLOCK_K, HD)
            s = lax.dot_general(k, q, NT, preferred_element_type=jnp.float32)
            for j in range(BLOCK_F):
                part = s[j * 128 : (j + 1) * 128].reshape(SEQ, 16, TILE_Q) + biases[j]
                buffer[side, j * 128 : (j + 1) * 128, :] = part.reshape(128, TILE_Q)
                top = jnp.maximum(top, jnp.max(part.reshape(16, 8, TILE_Q), axis=0))
        return top

    def mix(b, first, top, buffer, total):
        start = jnp.minimum(first + b * BLOCK_F, FRM - BLOCK_F)
        for side, ref in enumerate((own_ref, other_ref)):
            weights = jnp.exp2((buffer[side] - top) * COEF).astype(jnp.bfloat16)
            vt = [ref[start + j, 128 : 128 + LAT, :] for j in range(BLOCK_F)]
            vt = jnp.concatenate([jnp.concatenate(vt, axis=1), ones], axis=0)
            total = total + jnp.dot(vt, weights, preferred_element_type=jnp.float32)
        return total

    def store(rows, total):
        mixed = total[:LAT] / total[LAT : LAT + 1]
        done_ref[pl.ds(rows, TILE_Q), :] = jnp.concatenate([mixed, mixed], axis=0).T

    none = jnp.full((8, TILE_Q), FAR, jnp.float32)
    zero = jnp.zeros((LAT + 16, TILE_Q), jnp.float32)

    def pair(i, carry):
        tiles = [setup(GROUP * i + n) for n in range(GROUP)]
        one = tiles[0][4] == 1
        for n in range(1, GROUP):
            one = one & (tiles[n][4] == 1)

        @pl.when(one)
        def _():
            tops = []
            for n, (rows, q, q_clip, first, blocks) in enumerate(tiles):
                top = score(0, q, q_clip, first, s_ref.at[n], none)
                tops.append(jnp.max(top, axis=0, keepdims=True))
            for n, (rows, q, q_clip, first, blocks) in enumerate(tiles):
                store(rows, mix(0, first, tops[n], s_ref.at[n], zero))

        @pl.when(jnp.logical_not(one))
        def _():
            def single(n, carry):
                rows, q, q_clip, first, blocks = setup(GROUP * i + n)
                top = lax.fori_loop(
                    0, blocks, lambda b, top: score(b, q, q_clip, first, s_ref.at[b], top), none
                )
                top = jnp.max(top, axis=0, keepdims=True)
                store(
                    rows,
                    lax.fori_loop(
                        0, blocks, lambda b, total: mix(b, first, top, s_ref.at[b], total), zero
                    ),
                )
                return carry

            lax.fori_loop(0, GROUP, single, 0)

        return carry

    lax.fori_loop(0, TILES // GROUP, pair, 0)

    wide_low = lax.broadcasted_iota(jnp.int32, (FRAME_Q, HD), 1) < LAT
    for i in range(FRM // GATHER_F):
        packed = []
        for j in range(GATHER_F // 2):
            even = (i * GATHER_F + 2 * j) * FRAME_Q
            odd = even + FRAME_Q
            packed.append(
                jnp.where(wide_low, done_ref[even:odd, :], done_ref[odd : odd + FRAME_Q, :])
            )
        packed = jnp.concatenate(packed, axis=0).astype(jnp.bfloat16)
        placed = jnp.dot(place_ref[...], packed, preferred_element_type=jnp.float32)
        for s in range(SEQ):
            piece = placed[s * GATHER_R : (s + 1) * GATHER_R].astype(jnp.bfloat16)
            for halo in range(3):
                owner = s + 1 - halo
                if 0 <= owner < SEQ:
                    out_ref[owner, halo, i] = piece


def attend(meta, q, own, other):
    vmem = pl.BlockSpec(memory_space=pltpu.VMEM)
    return pl.pallas_call(
        attend_kernel,
        in_specs=[pl.BlockSpec(memory_space=pltpu.SMEM), vmem, vmem, vmem],
        out_specs=vmem,
        out_shape=pltpu.VMEM((SEQ, 3, FRM // GATHER_F, GATHER_R, HD), jnp.bfloat16),
        scratch_shapes=[
            pltpu.VMEM((max(GROUP, MAX_BLOCKS), 2, BLOCK_K, TILE_Q), jnp.float32),
            pltpu.VMEM((FRM * FRAME_Q, HD), jnp.float32),
            pltpu.VMEM((SEQ * GATHER_R, SEQ * GATHER_R), jnp.bfloat16),
        ],
        compiler_params=pltpu.CompilerParams(vmem_limit_bytes=24 * MIB),
    )(meta, q, own, other)


def merge_kernel(in_ref, widen_ref, out_ref):
    low = lax.broadcasted_iota(jnp.int32, (FRM // 2, 8, HD), 2) < LAT
    for halo in range(3):
        total = in_ref[0, halo].astype(jnp.float32)
        for head in range(1, SEQ):
            total = total + in_ref[head, halo].astype(jnp.float32)
        total = total.reshape(FRM // 2 * SHARE, HD).astype(jnp.bfloat16)
        total = jnp.dot(widen_ref[...], total, preferred_element_type=jnp.float32)
        total = total.reshape(FRM // 2, 8, HD)
        before = jnp.concatenate([total[:1], total[:-1]], axis=0)
        out_ref[:, 0, halo] = jnp.where(low, total, before).astype(jnp.bfloat16)
        out_ref[:, 1, halo] = total.astype(jnp.bfloat16)


def merge(parts):
    vmem = pl.BlockSpec(memory_space=pltpu.VMEM)
    widen = np.zeros((FRM // 2, 8, FRM // 2, SHARE), np.float32)
    for f in range(FRM // 2):
        for t in range(SHARE):
            widen[f, t, f, t] = 1
    widen = jnp.asarray(widen.reshape(FRM // 2 * 8, FRM // 2 * SHARE), jnp.bfloat16)
    return pl.pallas_call(
        merge_kernel,
        in_specs=[vmem, vmem],
        out_specs=vmem,
        out_shape=pltpu.VMEM((FRM // 2, 2, 3, 8, HD), jnp.bfloat16),
        compiler_params=pltpu.CompilerParams(vmem_limit_bytes=12 * MIB),
    )(parts, widen)


def assembly():
    out = np.zeros((3, 2, 3, 16, PARTS, 2, 3, 8), np.float32)
    for near in range(3):
        for token in range(16):
            source = token + near - 1
            if 0 <= source < 16:
                part = min(max(source - 1, 0) // STEP, PARTS - 1)
                for c in range(2):
                    for h in range(3):
                        out[near, c, h, token, part, c, h, source - part * STEP] = 1
    return out.reshape(3 * 96, 144)


def spreading():
    out = np.zeros((3, 2, 2, 2, LC, 2, 2, 2, 128), np.float32)
    for parity in range(2):
        for tap in range(3):
            column = parity + tap - 1
            near, b = 1 + column // 2, column % 2
            for pair in range(2):
                for a in range(2):
                    for ch in range(LC):
                        out[near, pair, a, b, ch, pair, a, parity, tap * LC + ch] = 1
    return out.reshape(3 * HD, 8 * 128)


def reordering():
    out = np.zeros((3, 16, 2, 2, 4, 2, 2, 4, 16), np.float32)
    for tap in range(3):
        for row in range(4):
            source = (row + tap + 1) // 2
            for frame in range(2):
                for parity in range(2):
                    for column in range(16):
                        out[tap, column, parity, frame, row, frame, parity, source, column] = 1
    return out.reshape(3, 256, 256)


def decode_kernel(
    clip_ref, place_ref, in_ref, gather_ref, spread_ref, order_ref, b_head_ref, w_in_hbm, b_in_ref,
    gain_ref, w_up_ref, b_up_ref, out_ref, w_in_ref, w_in_sem,
):
    w_in_copy = pltpu.make_async_copy(w_in_hbm, w_in_ref, w_in_sem)
    w_in_copy.start()
    first_frame = 2 * place_ref[0]
    core = lax.rem(place_ref[0], 2)
    no_above = place_ref[1] == 0
    no_below = place_ref[1] == SEQ - 1
    total = in_ref[0].astype(jnp.float32)
    for g in range(1, GROUPS):
        total = total + in_ref[g].astype(jnp.float32)
    total = total + b_head_ref[...]
    total = total.reshape(144, HD)
    total = jnp.where(core == 0, pltpu.roll(total, LAT, 1), total)
    row = lax.broadcasted_iota(jnp.int32, (144, HD), 0)
    patch = lax.rem(lax.shift_right_logical(row, 3), 3)
    outside = ((patch == 0) & no_above) | ((patch == 2) & no_below)
    tokens = jnp.where(outside, 0.0, total).astype(jnp.bfloat16)
    tokens = jnp.dot(gather_ref[...], tokens, preferred_element_type=jnp.float32)
    tokens = tokens.astype(jnp.bfloat16)
    near = jnp.concatenate([tokens[i * 96 : (i + 1) * 96] for i in range(3)], axis=1)
    cells = jnp.dot(near, spread_ref[...], preferred_element_type=jnp.float32).astype(jnp.bfloat16)

    w_in_copy.wait()
    hidden = jnp.zeros((256, C1), jnp.float32)
    for time_tap in (2, 1, 0):
        part = jnp.zeros((256, C1), jnp.float32)
        for row_tap in range(3):
            pieces = []
            for f in range(2):
                pair, c = divmod(f + time_tap, 2)
                for parity in range(2):
                    for r in range(4):
                        h, a = divmod(r + row_tap, 2)
                        e = (pair * 2 + a) * 2 + parity
                        rows = slice((c * 3 + h) * 16, (c * 3 + h + 1) * 16)
                        pieces.append(cells[rows, e * 128 : e * 128 + 3 * LC])
            columns = jnp.concatenate(pieces, axis=0)
            tap = (time_tap * 3 + row_tap) * 3 * LC
            part = part + jnp.dot(
                columns, w_in_ref[tap : tap + 3 * LC, :], preferred_element_type=jnp.float32
            )
        if time_tap == 2:
            hidden = part + b_in_ref[...]
        else:
            kept = []
            for f in range(2):
                earlier = first_frame + (f + time_tap - 2)
                same = clip_ref[jnp.maximum(earlier, 0)] == clip_ref[first_frame + f]
                keep = (earlier >= 0) & same
                kept.append(jnp.where(keep, part[f * 128 : (f + 1) * 128], 0.0))
            hidden = hidden + jnp.concatenate(kept, axis=0)
    mean_square = jnp.mean(hidden * hidden, axis=-1, keepdims=True)
    normed = hidden * lax.rsqrt(mean_square + 1e-06) * gain_ref[...]
    active = normed / (1.0 + jnp.exp(-normed))
    row = lax.broadcasted_iota(jnp.int32, (256, C1), 0)
    grid_row = lax.bitwise_and(lax.shift_right_logical(row, 4), 3)
    outside = ((grid_row == 0) & no_above) | ((grid_row == 3) & no_below)
    active = jnp.where(outside, 0.0, active).astype(jnp.bfloat16)

    taps = [jnp.zeros((256, CO), jnp.float32) for _ in range(3)]
    for row_tap in range(3):
        placed = jnp.dot(order_ref[row_tap], active, preferred_element_type=jnp.float32)
        placed = placed.astype(jnp.bfloat16)
        for col_tap in range(3):
            tap = (row_tap * 3 + col_tap) * C1
            taps[col_tap] = taps[col_tap] + lax.dot_general(
                placed, w_up_ref[:, tap : tap + C1], NT, preferred_element_type=jnp.float32
            )
    edge = jnp.zeros((8, CO), jnp.float32)
    before = jnp.concatenate([edge, taps[0][:-8]], axis=0)
    after = jnp.concatenate([taps[2][8:], edge], axis=0)
    even = before + taps[1] + taps[2] + b_up_ref[...]
    odd = taps[0] + taps[1] + after + b_up_ref[...]
    both = jnp.concatenate([even, odd], axis=1).astype(jnp.bfloat16).astype(jnp.float32)
    for column in range(32):
        piece = both[column * 8 : column * 8 + 8]
        lanes = slice(column * 2 * CO, (column + 1) * 2 * CO)
        out_ref[0, :, lanes] = piece[:4].astype(jnp.bfloat16)
        out_ref[1, :, lanes] = piece[4:].astype(jnp.bfloat16)


def decode(clip_ids, place, back, b_head, w_in, b_in, gain_in, w_up, b_up):
    vmem = pl.BlockSpec(memory_space=pltpu.VMEM)
    constants = [jnp.asarray(x, jnp.bfloat16) for x in (assembly(), spreading(), reordering())]
    return pl.pallas_call(
        decode_kernel,
        in_specs=[pl.BlockSpec(memory_space=pltpu.SMEM)] * 2
        + [vmem] * 5
        + [pl.BlockSpec(memory_space=pltpu.HBM)]
        + [vmem] * 4,
        out_specs=vmem,
        out_shape=jax.ShapeDtypeStruct((2, 4, 64 * CO), jnp.bfloat16),
        scratch_shapes=[pltpu.VMEM((27 * LC, C1), jnp.bfloat16), pltpu.SemaphoreType.DMA],
        compiler_params=pltpu.CompilerParams(vmem_limit_bytes=12 * MIB),
    )(
        clip_ids,
        place,
        back,
        *constants,
        jnp.concatenate([b_head, b_head])[None],
        pltpu.with_memory_space_constraint(w_in, pltpu.HBM),
        b_in[None],
        gain_in[None],
        w_up.T,
        b_up[None],
    )


def shards(queries, keys, values, clip_ids, w_head, b_head, w_in, b_in, gain_in, w_up, b_up):
    frame_position = lax.axis_index("frm")
    row_position = lax.axis_index("seq")
    core = lax.rem(frame_position, 2)

    slots = pack(queries, keys, values, w_head).reshape(FRM * SEQ, SLOT, HD)
    own = lax.all_to_all(slots, ("frm", "seq"), 0, 0, tiled=True)
    own_kv, own_q = prepare(own.reshape(FRM, SEQ, SLOT, HD))
    other_kv = lax.ppermute(own_kv, "frm", [(i, i ^ 1) for i in range(FRM)])

    below = jnp.sum(clip_ids[None, :] < clip_ids[:, None], axis=1, dtype=jnp.int32)
    upto = jnp.sum(clip_ids[None, :] <= clip_ids[:, None], axis=1, dtype=jnp.int32)
    kind = lax.broadcasted_iota(jnp.int32, (4, 2 * FRM), 0)
    meta = jnp.where(kind == 0, clip_ids, jnp.where(kind == 1, below, jnp.where(kind == 2, upto, core)))
    mixed = attend(meta, own_q, own_kv, other_kv).reshape(SEQ, -1, HD)
    by_row = lax.all_to_all(mixed, "seq", 0, 0, tiled=True)
    merged = merge(by_row.reshape(SEQ, 3, FRM // GATHER_F, GATHER_R, HD)).reshape(FRM, 24, HD)
    back = lax.all_to_all(merged, "frm", 0, 0, tiled=True)

    back = back[: 2 * PARTS * GROUPS].reshape(GROUPS, 2 * PARTS, 24, HD)
    place = jnp.where(jnp.arange(2) == 0, frame_position, row_position)
    return decode(clip_ids, place, back, b_head, w_in, b_in, gain_in, w_up, b_up)


def solution(mesh):
    in_specs = (
        P("frm", "seq", None),
        P("frm", "seq", None),
        P("frm", "seq", None),
        P(),
        P(),
        P(),
        P(),
        P(),
        P(),
        P(),
        P(),
    )
    out_specs = P("frm", "seq", None)
    return jax.shard_map(shards, mesh=mesh, in_specs=in_specs, out_specs=out_specs, check_vma=False)
```

```python
import functools
import math

import jax
import jax.numpy as jnp
import numpy as np
from jax import lax
from jax.experimental import pallas as pl
from jax.experimental.pallas import tpu as pltpu
from jax.sharding import PartitionSpec as P

HEADS = 40
HD = 128
LC = 16
C1 = 384
CO = 192
SEQ = 8
FRM = 32
GROUPS = 5
PARTS = 3
SHARE = 6
STEP = 5
SLOT = 32
LAT = 64
SPAN = SEQ * HD
FRAME_Q = SEQ * SHARE
GATHER_F = 8
GATHER_R = GATHER_F // 2 * SHARE
TILE_Q = 256
TILES = FRM * FRAME_Q // TILE_Q
TILE_SPAN = -(-TILE_Q // FRAME_Q) + 1
SIZES = (12, 17, 24, 32)
GROUP = 2
COEF = math.log2(math.e) / math.sqrt(HD)
FAR = -1e30
MIB = 1024 * 1024
NT = (((1,), (1,)), ((), ()))


def pack_kernel(q_hbm, k_hbm, v_hbm, w_hbm, out_ref, q_ref, k_ref, v_ref, w_ref, sems):
    copies = []
    for g in range(GROUPS):
        cols = slice(g * SPAN, (g + 1) * SPAN)
        group = []
        for i, (src, dst) in enumerate(
            ((v_hbm, v_ref), (k_hbm, k_ref), (q_hbm, q_ref), (w_hbm, w_ref))
        ):
            where = (slice(None), cols) if i == 3 else (slice(None), slice(None), cols)
            copy = pltpu.make_async_copy(src.at[where], dst.at[where], sems.at[g, i])
            copy.start()
            group.append(copy)
        copies.append(group)
    low = lax.broadcasted_iota(jnp.int32, (8, HD), 1) < LAT
    for g in range(GROUPS):
        for copy in copies[g]:
            copy.wait()
        for s in range(SEQ):
            cols = slice(g * SPAN + s * HD, g * SPAN + (s + 1) * HD)
            w = w_ref[:, cols]
            w2 = jnp.concatenate([w, w], axis=0)
            v = jnp.concatenate([v_ref[0, :, cols], v_ref[1, :, cols]], axis=0)
            proj = lax.dot_general(v, w2, NT, preferred_element_type=jnp.float32)
            keys = [k_ref[p, :, cols].astype(jnp.float32) for p in range(2)]
            for c in range(2):
                half = slice(c * 8, c * 8 + 8)
                k = jnp.concatenate([keys[0][half], keys[1][half]], axis=0).astype(jnp.bfloat16)
                packed = jnp.where(low, proj[c * 8 : c * 8 + 8], proj[16 + c * 8 : 24 + c * 8])
                q = q_ref[c, :, cols].astype(jnp.float32)
                for part in range(PARTS):
                    own = q if part == 0 else pltpu.roll(q, 16 - part * STEP, 0)
                    tail = jnp.concatenate([packed, own[:8]], axis=0)
                    out_ref[g * PARTS + part, c, s, 0:16, :] = k
                    out_ref[g * PARTS + part, c, s, 16:32, :] = tail.astype(jnp.bfloat16)


def pack(queries, keys, values, w_head):
    hbm = pl.BlockSpec(memory_space=pltpu.HBM)
    act = pltpu.VMEM((2, 16, HEADS * HD), jnp.bfloat16)
    return pl.pallas_call(
        pack_kernel,
        in_specs=[hbm, hbm, hbm, hbm],
        out_specs=pl.BlockSpec(memory_space=pltpu.VMEM),
        out_shape=pltpu.VMEM((FRM // 2, 2, SEQ, SLOT, HD), jnp.bfloat16),
        scratch_shapes=[
            act,
            act,
            act,
            pltpu.VMEM((LAT, HEADS * HD), jnp.bfloat16),
            pltpu.SemaphoreType.DMA((GROUPS, 4)),
        ],
        compiler_params=pltpu.CompilerParams(vmem_limit_bytes=12 * MIB),
    )(*(pltpu.with_memory_space_constraint(x, pltpu.HBM) for x in (queries, keys, values, w_head.T)))


def prepare_kernel(in_ref, kv_ref, q_ref, pick_ref):
    row = lax.broadcasted_iota(jnp.int32, (2 * FRAME_Q, 256), 0)
    col = lax.broadcasted_iota(jnp.int32, (2 * FRAME_Q, 256), 1)
    inner = lax.bitwise_and(col, 15) - 8
    hit = (row == SHARE * lax.shift_right_logical(col, 4) + inner) & (inner >= 0) & (inner < SHARE)
    pick_ref[...] = jnp.where(hit, 1.0, 0.0).astype(jnp.bfloat16)

    def body(i, carry):
        for j in range(2):
            f = 2 * i + j
            kv_ref[f, 0:128, :] = in_ref[f, :, 0:16, :].reshape(128, HD)
            packed = in_ref[f, :, 16:32, :].astype(jnp.float32)[:, :8]
            rolled = pltpu.roll(packed.reshape(SEQ * 8, HD), LAT, 1).reshape(SEQ, 8, HD)
            block = jnp.concatenate([packed, rolled], axis=1).reshape(128, HD).T
            kv_ref[f, 128:192, :] = block[:LAT].astype(jnp.bfloat16)
        q = in_ref[pl.ds(2 * i, 2), :, 16:32, :].reshape(256, HD)
        q = jnp.dot(pick_ref[...], q, preferred_element_type=jnp.float32)
        rows = pl.multiple_of(i * 2 * FRAME_Q, 2 * FRAME_Q)
        q_ref[pl.ds(rows, 2 * FRAME_Q), :] = q.astype(jnp.bfloat16)
        return carry

    lax.fori_loop(0, FRM // 2, body, 0, unroll=16)


def prepare(own):
    vmem = pl.BlockSpec(memory_space=pltpu.VMEM)
    return pl.pallas_call(
        prepare_kernel,
        in_specs=[vmem],
        out_specs=[vmem, vmem],
        out_shape=[
            pltpu.VMEM((FRM, 128 + LAT, HD), jnp.bfloat16),
            pltpu.VMEM((FRM * FRAME_Q, HD), jnp.bfloat16),
        ],
        scratch_shapes=[pltpu.VMEM((2 * FRAME_Q, 256), jnp.bfloat16)],
        compiler_params=pltpu.CompilerParams(vmem_limit_bytes=12 * MIB),
    )(own)


def attend_kernel(
    meta_ref, q_ref, own_ref, other_ref, w_in_hbm, out_ref, w_in_ref, s_ref, done_ref, place_ref, w_in_sem
):
    core = meta_ref[3, 0]
    w_in_copy = pltpu.make_async_copy(w_in_hbm, w_in_ref, w_in_sem)
    w_in_copy.start()
    share = lax.broadcasted_iota(jnp.int32, (SEQ * GATHER_R, 1), 0)
    source = jnp.zeros_like(share)
    for size, unit, stop in ((GATHER_R, SHARE, SEQ), (SHARE, FRAME_Q, GATHER_F // 2)):
        count = jnp.zeros_like(share)
        for i in range(1, stop):
            count = count + jnp.where(share >= size * i, 1, 0)
        share = share - count * size
        source = source + count * unit
    col = lax.broadcasted_iota(jnp.int32, (SEQ * GATHER_R, SEQ * GATHER_R), 1)
    place_ref[...] = jnp.where(col == source + share, 1.0, 0.0).astype(jnp.bfloat16)
    ones = jnp.ones((16, FRM * 128), jnp.bfloat16)
    lane = lax.broadcasted_iota(jnp.int32, (8, TILE_Q), 1)

    def setup(t):
        rows = pl.multiple_of(t * TILE_Q, TILE_Q)
        q = q_ref[pl.ds(rows, TILE_Q), :]
        begin_f = lax.div(rows, FRAME_Q)
        end_f = lax.div(rows + (TILE_Q - 1), FRAME_Q)
        first = lax.shift_right_logical(meta_ref[1, 2 * begin_f + core], 1)
        last = lax.shift_right_logical(meta_ref[2, 2 * end_f + core] + 1, 1)
        q_clip = jnp.zeros((8, TILE_Q), jnp.int32)
        for j in range(TILE_SPAN):
            f = begin_f + j
            clip = meta_ref[0, jnp.minimum(2 * f + core, 2 * FRM - 1)]
            q_clip = jnp.where(lane + rows >= f * FRAME_Q, clip, q_clip)
        return rows, q, q_clip, first, last - first

    def score(size, q, q_clip, first, buffer):
        start = jnp.minimum(first, FRM - size)
        top = jnp.full((8, TILE_Q), FAR, jnp.float32)
        biases = []
        for j in range(size):
            pair = []
            for p in range(2):
                clip = meta_ref[0, 2 * (start + j) + p]
                pair.append(jnp.where(q_clip == clip, 0.0, FAR))
            biases.append(jnp.concatenate(pair, axis=0)[None])
        for side, ref in enumerate((own_ref, other_ref)):
            k = ref[pl.ds(start, size), 0:128, :].reshape(size * 128, HD)
            s = lax.dot_general(k, q, NT, preferred_element_type=jnp.float32)
            for j in range(size):
                part = s[j * 128 : (j + 1) * 128].reshape(SEQ, 16, TILE_Q) + biases[j]
                buffer[side, j * 128 : (j + 1) * 128, :] = part.reshape(128, TILE_Q)
                top = jnp.maximum(top, jnp.max(part.reshape(16, 8, TILE_Q), axis=0))
        return top

    def mix(size, first, top, buffer):
        start = jnp.minimum(first, FRM - size)
        total = jnp.zeros((LAT + 16, TILE_Q), jnp.float32)
        for side, ref in enumerate((own_ref, other_ref)):
            weights = jnp.exp2((buffer[side, : size * 128] - top) * COEF).astype(jnp.bfloat16)
            vt = [ref[start + j, 128 : 128 + LAT, :] for j in range(size)]
            vt = jnp.concatenate([jnp.concatenate(vt, axis=1), ones[:, : size * 128]], axis=0)
            total = total + jnp.dot(vt, weights, preferred_element_type=jnp.float32)
        return total

    def store(rows, total):
        mixed = total[:LAT] / total[LAT : LAT + 1]
        done_ref[pl.ds(rows, TILE_Q), :] = jnp.concatenate([mixed, mixed], axis=0).T

    def pair(i, carry):
        tiles = [setup(GROUP * i + n) for n in range(GROUP)]
        widest = tiles[0][4]
        for n in range(1, GROUP):
            widest = jnp.maximum(widest, tiles[n][4])

        def together(size):
            tops = []
            for n, (rows, q, q_clip, first, span) in enumerate(tiles):
                top = score(size, q, q_clip, first, s_ref.at[n])
                tops.append(jnp.max(top, axis=0, keepdims=True))
            for n, (rows, q, q_clip, first, span) in enumerate(tiles):
                store(rows, mix(size, first, tops[n], s_ref.at[n]))

        for below, size in zip((0,) + SIZES, SIZES):
            fits = (widest > below) & (widest <= size)
            pl.when(fits)(functools.partial(together, size))
        return carry

    lax.fori_loop(0, TILES // GROUP, pair, 0)

    wide_low = lax.broadcasted_iota(jnp.int32, (FRAME_Q, HD), 1) < LAT
    for i in range(FRM // GATHER_F):
        packed = []
        for j in range(GATHER_F // 2):
            even = (i * GATHER_F + 2 * j) * FRAME_Q
            odd = even + FRAME_Q
            packed.append(
                jnp.where(wide_low, done_ref[even:odd, :], done_ref[odd : odd + FRAME_Q, :])
            )
        packed = jnp.concatenate(packed, axis=0).astype(jnp.bfloat16)
        placed = jnp.dot(place_ref[...], packed, preferred_element_type=jnp.float32)
        for s in range(SEQ):
            piece = placed[s * GATHER_R : (s + 1) * GATHER_R].astype(jnp.bfloat16)
            for halo in range(3):
                owner = s + 1 - halo
                if 0 <= owner < SEQ:
                    out_ref[owner, halo, i] = piece
    w_in_copy.wait()


def attend(meta, q, own, other, w_in):
    vmem = pl.BlockSpec(memory_space=pltpu.VMEM)
    return pl.pallas_call(
        attend_kernel,
        in_specs=[
            pl.BlockSpec(memory_space=pltpu.SMEM),
            vmem,
            vmem,
            vmem,
            pl.BlockSpec(memory_space=pltpu.HBM),
        ],
        out_specs=[vmem, vmem],
        out_shape=[
            pltpu.VMEM((SEQ, 3, FRM // GATHER_F, GATHER_R, HD), jnp.bfloat16),
            pltpu.VMEM(w_in.shape, jnp.bfloat16),
        ],
        scratch_shapes=[
            pltpu.VMEM((GROUP, 2, FRM * 128, TILE_Q), jnp.float32),
            pltpu.VMEM((FRM * FRAME_Q, HD), jnp.float32),
            pltpu.VMEM((SEQ * GATHER_R, SEQ * GATHER_R), jnp.bfloat16),
            pltpu.SemaphoreType.DMA,
        ],
        compiler_params=pltpu.CompilerParams(vmem_limit_bytes=36 * MIB),
    )(meta, q, own, other, pltpu.with_memory_space_constraint(w_in, pltpu.HBM))


def merge_kernel(in_ref, widen_ref, out_ref):
    low = lax.broadcasted_iota(jnp.int32, (FRM // 2, 8, HD), 2) < LAT
    for halo in range(3):
        total = in_ref[0, halo].astype(jnp.float32)
        for head in range(1, SEQ):
            total = total + in_ref[head, halo].astype(jnp.float32)
        total = total.reshape(FRM // 2 * SHARE, HD).astype(jnp.bfloat16)
        total = jnp.dot(widen_ref[...], total, preferred_element_type=jnp.float32)
        total = total.reshape(FRM // 2, 8, HD)
        before = jnp.concatenate([total[:1], total[:-1]], axis=0)
        out_ref[:, 0, halo] = jnp.where(low, total, before).astype(jnp.bfloat16)
        out_ref[:, 1, halo] = total.astype(jnp.bfloat16)


def merge(parts):
    vmem = pl.BlockSpec(memory_space=pltpu.VMEM)
    widen = np.zeros((FRM // 2, 8, FRM // 2, SHARE), np.float32)
    for f in range(FRM // 2):
        for t in range(SHARE):
            widen[f, t, f, t] = 1
    widen = jnp.asarray(widen.reshape(FRM // 2 * 8, FRM // 2 * SHARE), jnp.bfloat16)
    return pl.pallas_call(
        merge_kernel,
        in_specs=[vmem, vmem],
        out_specs=vmem,
        out_shape=pltpu.VMEM((FRM // 2, 2, 3, 8, HD), jnp.bfloat16),
        compiler_params=pltpu.CompilerParams(vmem_limit_bytes=12 * MIB),
    )(parts, widen)


def assembly():
    out = np.zeros((3, 2, 3, 16, PARTS, 2, 3, 8), np.float32)
    for near in range(3):
        for token in range(16):
            source = token + near - 1
            if 0 <= source < 16:
                part = min(max(source - 1, 0) // STEP, PARTS - 1)
                for c in range(2):
                    for h in range(3):
                        out[near, c, h, token, part, c, h, source - part * STEP] = 1
    return out.reshape(3 * 96, 144)


def spreading():
    out = np.zeros((3, 2, 2, 2, LC, 2, 2, 2, 128), np.float32)
    for parity in range(2):
        for tap in range(3):
            column = parity + tap - 1
            near, b = 1 + column // 2, column % 2
            for pair in range(2):
                for a in range(2):
                    for ch in range(LC):
                        out[near, pair, a, b, ch, pair, a, parity, tap * LC + ch] = 1
    return out.reshape(3 * HD, 8 * 128)


def reordering():
    out = np.zeros((3, 16, 2, 2, 4, 2, 2, 4, 16), np.float32)
    for tap in range(3):
        for row in range(4):
            source = (row + tap + 1) // 2
            for frame in range(2):
                for parity in range(2):
                    for column in range(16):
                        out[tap, column, parity, frame, row, frame, parity, source, column] = 1
    return out.reshape(3, 256, 256)


def decode_kernel(
    clip_ref, place_ref, in_ref, gather_ref, spread_ref, order_ref, b_head_ref, w_in_ref, b_in_ref,
    gain_ref, w_up_ref, b_up_ref, out_ref,
):
    first_frame = 2 * place_ref[0]
    core = lax.rem(place_ref[0], 2)
    no_above = place_ref[1] == 0
    no_below = place_ref[1] == SEQ - 1
    total = in_ref[0].astype(jnp.float32)
    for g in range(1, GROUPS):
        total = total + in_ref[g].astype(jnp.float32)
    total = total + b_head_ref[...]
    total = total.reshape(144, HD)
    total = jnp.where(core == 0, pltpu.roll(total, LAT, 1), total)
    row = lax.broadcasted_iota(jnp.int32, (144, HD), 0)
    patch = lax.rem(lax.shift_right_logical(row, 3), 3)
    outside = ((patch == 0) & no_above) | ((patch == 2) & no_below)
    tokens = jnp.where(outside, 0.0, total).astype(jnp.bfloat16)
    tokens = jnp.dot(gather_ref[...], tokens, preferred_element_type=jnp.float32)
    tokens = tokens.astype(jnp.bfloat16)
    near = jnp.concatenate([tokens[i * 96 : (i + 1) * 96] for i in range(3)], axis=1)
    cells = jnp.dot(near, spread_ref[...], preferred_element_type=jnp.float32).astype(jnp.bfloat16)

    hidden = jnp.zeros((256, C1), jnp.float32)
    for time_tap in (2, 1, 0):
        part = jnp.zeros((256, C1), jnp.float32)
        for row_tap in range(3):
            pieces = []
            for f in range(2):
                pair, c = divmod(f + time_tap, 2)
                for parity in range(2):
                    for r in range(4):
                        h, a = divmod(r + row_tap, 2)
                        e = (pair * 2 + a) * 2 + parity
                        rows = slice((c * 3 + h) * 16, (c * 3 + h + 1) * 16)
                        pieces.append(cells[rows, e * 128 : e * 128 + 3 * LC])
            columns = jnp.concatenate(pieces, axis=0)
            tap = (time_tap * 3 + row_tap) * 3 * LC
            part = part + jnp.dot(
                columns, w_in_ref[tap : tap + 3 * LC, :], preferred_element_type=jnp.float32
            )
        if time_tap == 2:
            hidden = part + b_in_ref[...]
        else:
            kept = []
            for f in range(2):
                earlier = first_frame + (f + time_tap - 2)
                same = clip_ref[jnp.maximum(earlier, 0)] == clip_ref[first_frame + f]
                keep = (earlier >= 0) & same
                kept.append(jnp.where(keep, part[f * 128 : (f + 1) * 128], 0.0))
            hidden = hidden + jnp.concatenate(kept, axis=0)
    mean_square = jnp.mean(hidden * hidden, axis=-1, keepdims=True)
    normed = hidden * lax.rsqrt(mean_square + 1e-06) * gain_ref[...]
    active = normed / (1.0 + jnp.exp(-normed))
    row = lax.broadcasted_iota(jnp.int32, (256, C1), 0)
    grid_row = lax.bitwise_and(lax.shift_right_logical(row, 4), 3)
    outside = ((grid_row == 0) & no_above) | ((grid_row == 3) & no_below)
    active = jnp.where(outside, 0.0, active).astype(jnp.bfloat16)

    taps = [jnp.zeros((256, CO), jnp.float32) for _ in range(3)]
    for row_tap in range(3):
        placed = jnp.dot(order_ref[row_tap], active, preferred_element_type=jnp.float32)
        placed = placed.astype(jnp.bfloat16)
        for col_tap in range(3):
            tap = (row_tap * 3 + col_tap) * C1
            taps[col_tap] = taps[col_tap] + lax.dot_general(
                placed, w_up_ref[:, tap : tap + C1], NT, preferred_element_type=jnp.float32
            )
    edge = jnp.zeros((8, CO), jnp.float32)
    before = jnp.concatenate([edge, taps[0][:-8]], axis=0)
    after = jnp.concatenate([taps[2][8:], edge], axis=0)
    even = before + taps[1] + taps[2] + b_up_ref[...]
    odd = taps[0] + taps[1] + after + b_up_ref[...]
    both = jnp.concatenate([even, odd], axis=1).astype(jnp.bfloat16).astype(jnp.float32)
    for column in range(32):
        piece = both[column * 8 : column * 8 + 8]
        lanes = slice(column * 2 * CO, (column + 1) * 2 * CO)
        out_ref[0, :, lanes] = piece[:4].astype(jnp.bfloat16)
        out_ref[1, :, lanes] = piece[4:].astype(jnp.bfloat16)


def decode(clip_ids, place, back, b_head, w_in, b_in, gain_in, w_up, b_up):
    vmem = pl.BlockSpec(memory_space=pltpu.VMEM)
    constants = [jnp.asarray(x, jnp.bfloat16) for x in (assembly(), spreading(), reordering())]
    return pl.pallas_call(
        decode_kernel,
        in_specs=[pl.BlockSpec(memory_space=pltpu.SMEM)] * 2 + [vmem] * 10,
        out_specs=vmem,
        out_shape=jax.ShapeDtypeStruct((2, 4, 64 * CO), jnp.bfloat16),
        compiler_params=pltpu.CompilerParams(vmem_limit_bytes=12 * MIB),
    )(
        clip_ids,
        place,
        back,
        *constants,
        jnp.concatenate([b_head, b_head])[None],
        w_in,
        b_in[None],
        gain_in[None],
        w_up.T,
        b_up[None],
    )


def shards(queries, keys, values, clip_ids, w_head, b_head, w_in, b_in, gain_in, w_up, b_up):
    frame_position = lax.axis_index("frm")
    row_position = lax.axis_index("seq")
    core = lax.rem(frame_position, 2)

    slots = pack(queries, keys, values, w_head).reshape(FRM * SEQ, SLOT, HD)
    own = lax.all_to_all(slots, ("frm", "seq"), 0, 0, tiled=True)
    own_kv, own_q = prepare(own.reshape(FRM, SEQ, SLOT, HD))
    other_kv = lax.ppermute(own_kv, "frm", [(i, i ^ 1) for i in range(FRM)])

    below = jnp.sum(clip_ids[None, :] < clip_ids[:, None], axis=1, dtype=jnp.int32)
    upto = jnp.sum(clip_ids[None, :] <= clip_ids[:, None], axis=1, dtype=jnp.int32)
    kind = lax.broadcasted_iota(jnp.int32, (4, 2 * FRM), 0)
    meta = jnp.where(kind == 0, clip_ids, jnp.where(kind == 1, below, jnp.where(kind == 2, upto, core)))
    mixed, w_in = attend(meta, own_q, own_kv, other_kv, w_in)
    by_row = lax.all_to_all(mixed.reshape(SEQ, -1, HD), "seq", 0, 0, tiled=True)
    merged = merge(by_row.reshape(SEQ, 3, FRM // GATHER_F, GATHER_R, HD)).reshape(FRM, 24, HD)
    back = lax.all_to_all(merged, "frm", 0, 0, tiled=True)

    back = back[: 2 * PARTS * GROUPS].reshape(GROUPS, 2 * PARTS, 24, HD)
    place = jnp.where(jnp.arange(2) == 0, frame_position, row_position)
    return decode(clip_ids, place, back, b_head, w_in, b_in, gain_in, w_up, b_up)


def solution(mesh):
    in_specs = (
        P("frm", "seq", None),
        P("frm", "seq", None),
        P("frm", "seq", None),
        P(),
        P(),
        P(),
        P(),
        P(),
        P(),
        P(),
        P(),
    )
    out_specs = P("frm", "seq", None)
    return jax.shard_map(shards, mesh=mesh, in_specs=in_specs, out_specs=out_specs, check_vma=False)
```

```python
import functools
import math

import jax
import jax.numpy as jnp
import numpy as np
from jax import lax
from jax.experimental import pallas as pl
from jax.experimental.pallas import tpu as pltpu
from jax.sharding import PartitionSpec as P

HEADS = 40
HD = 128
LC = 16
C1 = 384
CO = 192
SEQ = 8
FRM = 32
GROUPS = 5
PARTS = 3
SHARE = 6
STEP = 5
SLOT = 32
LAT = 64
SPAN = SEQ * HD
FRAME_Q = SEQ * SHARE
GATHER_F = 8
GATHER_R = GATHER_F // 2 * SHARE
TILE_Q = 256
TILES = FRM * FRAME_Q // TILE_Q
TILE_SPAN = -(-TILE_Q // FRAME_Q) + 1
SIZES = (12, 17, 22, 27, 32)
GROUP = 2
COEF = math.log2(math.e) / math.sqrt(HD)
FAR = -1e30
MIB = 1024 * 1024
NT = (((1,), (1,)), ((), ()))


def pack_kernel(q_hbm, k_hbm, v_hbm, w_hbm, out_ref, q_ref, k_ref, v_ref, w_ref, sems):
    copies = []
    for g in range(GROUPS):
        cols = slice(g * SPAN, (g + 1) * SPAN)
        group = []
        for i, (src, dst) in enumerate(
            ((v_hbm, v_ref), (k_hbm, k_ref), (q_hbm, q_ref), (w_hbm, w_ref))
        ):
            where = (slice(None), cols) if i == 3 else (slice(None), slice(None), cols)
            copy = pltpu.make_async_copy(src.at[where], dst.at[where], sems.at[g, i])
            copy.start()
            group.append(copy)
        copies.append(group)
    low = lax.broadcasted_iota(jnp.int32, (8, HD), 1) < LAT
    for g in range(GROUPS):
        for copy in copies[g]:
            copy.wait()
        for s in range(SEQ):
            cols = slice(g * SPAN + s * HD, g * SPAN + (s + 1) * HD)
            w = w_ref[:, cols]
            w2 = jnp.concatenate([w, w], axis=0)
            v = jnp.concatenate([v_ref[0, :, cols], v_ref[1, :, cols]], axis=0)
            proj = lax.dot_general(v, w2, NT, preferred_element_type=jnp.float32)
            keys = [k_ref[p, :, cols].astype(jnp.float32) for p in range(2)]
            for c in range(2):
                half = slice(c * 8, c * 8 + 8)
                k = jnp.concatenate([keys[0][half], keys[1][half]], axis=0).astype(jnp.bfloat16)
                packed = jnp.where(low, proj[c * 8 : c * 8 + 8], proj[16 + c * 8 : 24 + c * 8])
                q = q_ref[c, :, cols].astype(jnp.float32)
                for part in range(PARTS):
                    own = q if part == 0 else pltpu.roll(q, 16 - part * STEP, 0)
                    tail = jnp.concatenate([packed, own[:8]], axis=0)
                    out_ref[s, g * PARTS + part, c, 0:16, :] = k
                    out_ref[s, g * PARTS + part, c, 16:32, :] = tail.astype(jnp.bfloat16)


def pack(queries, keys, values, w_head):
    hbm = pl.BlockSpec(memory_space=pltpu.HBM)
    act = pltpu.VMEM((2, 16, HEADS * HD), jnp.bfloat16)
    return pl.pallas_call(
        pack_kernel,
        in_specs=[hbm, hbm, hbm, hbm],
        out_specs=pl.BlockSpec(memory_space=pltpu.VMEM),
        out_shape=pltpu.VMEM((SEQ, FRM // 2, 2, SLOT, HD), jnp.bfloat16),
        scratch_shapes=[
            act,
            act,
            act,
            pltpu.VMEM((LAT, HEADS * HD), jnp.bfloat16),
            pltpu.SemaphoreType.DMA((GROUPS, 4)),
        ],
        compiler_params=pltpu.CompilerParams(vmem_limit_bytes=12 * MIB),
    )(*(pltpu.with_memory_space_constraint(x, pltpu.HBM) for x in (queries, keys, values, w_head.T)))


def prepare_kernel(in_ref, kv_ref, q_ref, pick_ref):
    row = lax.broadcasted_iota(jnp.int32, (2 * FRAME_Q, 256), 0)
    col = lax.broadcasted_iota(jnp.int32, (2 * FRAME_Q, 256), 1)
    inner = lax.bitwise_and(col, 15) - 8
    hit = (row == SHARE * lax.shift_right_logical(col, 4) + inner) & (inner >= 0) & (inner < SHARE)
    pick_ref[...] = jnp.where(hit, 1.0, 0.0).astype(jnp.bfloat16)

    def body(i, carry):
        for j in range(2):
            f = 2 * i + j
            kv_ref[f, 0:128, :] = in_ref[:, f, 0:16, :].reshape(128, HD)
            packed = in_ref[:, f, 16:32, :].astype(jnp.float32)[:, :8]
            rolled = pltpu.roll(packed.reshape(SEQ * 8, HD), LAT, 1).reshape(SEQ, 8, HD)
            block = jnp.concatenate([packed, rolled], axis=1).reshape(128, HD).T
            kv_ref[f, 128:192, :] = block[:LAT].astype(jnp.bfloat16)
        q = [in_ref[:, 2 * i + j, 16:32, :].reshape(128, HD) for j in range(2)]
        q = jnp.concatenate(q, axis=0)
        q = jnp.dot(pick_ref[...], q, preferred_element_type=jnp.float32)
        rows = pl.multiple_of(i * 2 * FRAME_Q, 2 * FRAME_Q)
        q_ref[pl.ds(rows, 2 * FRAME_Q), :] = q.astype(jnp.bfloat16)
        return carry

    lax.fori_loop(0, FRM // 2, body, 0, unroll=16)


def prepare(own):
    vmem = pl.BlockSpec(memory_space=pltpu.VMEM)
    return pl.pallas_call(
        prepare_kernel,
        in_specs=[vmem],
        out_specs=[vmem, vmem],
        out_shape=[
            pltpu.VMEM((FRM, 128 + LAT, HD), jnp.bfloat16),
            pltpu.VMEM((FRM * FRAME_Q, HD), jnp.bfloat16),
        ],
        scratch_shapes=[pltpu.VMEM((2 * FRAME_Q, 256), jnp.bfloat16)],
        compiler_params=pltpu.CompilerParams(vmem_limit_bytes=12 * MIB),
    )(own)


def attend_kernel(meta_ref, q_ref, own_ref, other_ref, out_ref, s_ref, done_ref, place_ref):
    core = meta_ref[3, 0]
    share = lax.broadcasted_iota(jnp.int32, (SEQ * GATHER_R, 1), 0)
    source = jnp.zeros_like(share)
    for size, unit, stop in ((GATHER_R, SHARE, SEQ), (SHARE, FRAME_Q, GATHER_F // 2)):
        count = jnp.zeros_like(share)
        for i in range(1, stop):
            count = count + jnp.where(share >= size * i, 1, 0)
        share = share - count * size
        source = source + count * unit
    col = lax.broadcasted_iota(jnp.int32, (SEQ * GATHER_R, SEQ * GATHER_R), 1)
    place_ref[...] = jnp.where(col == source + share, 1.0, 0.0).astype(jnp.bfloat16)
    ones = jnp.ones((16, FRM * 128), jnp.bfloat16)
    lane = lax.broadcasted_iota(jnp.int32, (8, TILE_Q), 1)

    def setup(t):
        rows = pl.multiple_of(t * TILE_Q, TILE_Q)
        q = q_ref[pl.ds(rows, TILE_Q), :]
        begin_f = lax.div(rows, FRAME_Q)
        end_f = lax.div(rows + (TILE_Q - 1), FRAME_Q)
        first = lax.shift_right_logical(meta_ref[1, 2 * begin_f + core], 1)
        last = lax.shift_right_logical(meta_ref[2, 2 * end_f + core] + 1, 1)
        q_clip = jnp.zeros((8, TILE_Q), jnp.int32)
        for j in range(TILE_SPAN):
            f = begin_f + j
            clip = meta_ref[0, jnp.minimum(2 * f + core, 2 * FRM - 1)]
            q_clip = jnp.where(lane + rows >= f * FRAME_Q, clip, q_clip)
        return rows, q, q_clip, first, last - first

    def score(size, q, q_clip, first, buffer):
        start = jnp.minimum(first, FRM - size)
        top = jnp.full((8, TILE_Q), FAR, jnp.float32)
        biases = []
        for j in range(size):
            pair = []
            for p in range(2):
                clip = meta_ref[0, 2 * (start + j) + p]
                pair.append(jnp.where(q_clip == clip, 0.0, FAR))
            biases.append(jnp.concatenate(pair, axis=0)[None])
        for side, ref in enumerate((own_ref, other_ref)):
            k = ref[pl.ds(start, size), 0:128, :].reshape(size * 128, HD)
            s = lax.dot_general(k, q, NT, preferred_element_type=jnp.float32)
            for j in range(size):
                part = s[j * 128 : (j + 1) * 128].reshape(SEQ, 16, TILE_Q) + biases[j]
                buffer[side, j * 128 : (j + 1) * 128, :] = part.reshape(128, TILE_Q)
                top = jnp.maximum(top, jnp.max(part.reshape(16, 8, TILE_Q), axis=0))
        return top

    def mix(size, first, top, buffer):
        start = jnp.minimum(first, FRM - size)
        total = jnp.zeros((LAT + 16, TILE_Q), jnp.float32)
        for side, ref in enumerate((own_ref, other_ref)):
            weights = jnp.exp2((buffer[side, : size * 128] - top) * COEF).astype(jnp.bfloat16)
            vt = [ref[start + j, 128 : 128 + LAT, :] for j in range(size)]
            vt = jnp.concatenate([jnp.concatenate(vt, axis=1), ones[:, : size * 128]], axis=0)
            total = total + jnp.dot(vt, weights, preferred_element_type=jnp.float32)
        return total

    def store(rows, total):
        mixed = total[:LAT] / total[LAT : LAT + 1]
        done_ref[pl.ds(rows, TILE_Q), :] = jnp.concatenate([mixed, mixed], axis=0).T

    def pair(i, carry):
        tiles = [setup(GROUP * i + n) for n in range(GROUP)]
        widest = tiles[0][4]
        for n in range(1, GROUP):
            widest = jnp.maximum(widest, tiles[n][4])

        def together(size):
            tops = []
            for n, (rows, q, q_clip, first, span) in enumerate(tiles):
                top = score(size, q, q_clip, first, s_ref.at[n])
                tops.append(jnp.max(top, axis=0, keepdims=True))
            for n, (rows, q, q_clip, first, span) in enumerate(tiles):
                store(rows, mix(size, first, tops[n], s_ref.at[n]))

        for below, size in zip((0,) + SIZES, SIZES):
            fits = (widest > below) & (widest <= size)
            pl.when(fits)(functools.partial(together, size))
        return carry

    lax.fori_loop(0, TILES // GROUP, pair, 0)

    wide_low = lax.broadcasted_iota(jnp.int32, (FRAME_Q, HD), 1) < LAT
    for i in range(FRM // GATHER_F):
        packed = []
        for j in range(GATHER_F // 2):
            even = (i * GATHER_F + 2 * j) * FRAME_Q
            odd = even + FRAME_Q
            packed.append(
                jnp.where(wide_low, done_ref[even:odd, :], done_ref[odd : odd + FRAME_Q, :])
            )
        packed = jnp.concatenate(packed, axis=0).astype(jnp.bfloat16)
        placed = jnp.dot(place_ref[...], packed, preferred_element_type=jnp.float32)
        for s in range(SEQ):
            piece = placed[s * GATHER_R : (s + 1) * GATHER_R].astype(jnp.bfloat16)
            for halo in range(3):
                owner = s + 1 - halo
                if 0 <= owner < SEQ:
                    out_ref[owner, halo, i] = piece


def attend(meta, q, own, other):
    vmem = pl.BlockSpec(memory_space=pltpu.VMEM)
    return pl.pallas_call(
        attend_kernel,
        in_specs=[
            pl.BlockSpec(memory_space=pltpu.SMEM),
            vmem,
            vmem,
            vmem,
        ],
        out_specs=vmem,
        out_shape=pltpu.VMEM((SEQ, 3, FRM // GATHER_F, GATHER_R, HD), jnp.bfloat16),
        scratch_shapes=[
            pltpu.VMEM((GROUP, 2, FRM * 128, TILE_Q), jnp.float32),
            pltpu.VMEM((FRM * FRAME_Q, HD), jnp.float32),
            pltpu.VMEM((SEQ * GATHER_R, SEQ * GATHER_R), jnp.bfloat16),
        ],
        compiler_params=pltpu.CompilerParams(vmem_limit_bytes=36 * MIB),
    )(meta, q, own, other)


def merge_kernel(in_ref, out_ref):
    low = lax.broadcasted_iota(jnp.int32, (FRM // 2, 8, HD), 2) < LAT
    row = lax.broadcasted_iota(jnp.int32, (FRM // 2 * 8, FRM // 2 * SHARE), 0)
    col = lax.broadcasted_iota(jnp.int32, (FRM // 2 * 8, FRM // 2 * SHARE), 1)
    share = lax.bitwise_and(row, 7)
    hit = (col == SHARE * lax.shift_right_logical(row, 3) + share) & (share < SHARE)
    widen = jnp.where(hit, 1.0, 0.0).astype(jnp.bfloat16)
    for halo in range(3):
        total = in_ref[0, halo].astype(jnp.float32)
        for head in range(1, SEQ):
            total = total + in_ref[head, halo].astype(jnp.float32)
        total = total.reshape(FRM // 2 * SHARE, HD).astype(jnp.bfloat16)
        total = jnp.dot(widen, total, preferred_element_type=jnp.float32)
        total = total.reshape(FRM // 2, 8, HD)
        before = jnp.concatenate([total[:1], total[:-1]], axis=0)
        out_ref[:, 0, halo] = jnp.where(low, total, before).astype(jnp.bfloat16)
        out_ref[:, 1, halo] = total.astype(jnp.bfloat16)


def merge(parts):
    vmem = pl.BlockSpec(memory_space=pltpu.VMEM)
    return pl.pallas_call(
        merge_kernel,
        in_specs=[vmem],
        out_specs=vmem,
        out_shape=pltpu.VMEM((FRM // 2, 2, 3, 8, HD), jnp.bfloat16),
        compiler_params=pltpu.CompilerParams(vmem_limit_bytes=12 * MIB),
    )(parts)


def assembly():
    out = np.zeros((3, 2, 3, 16, PARTS, 2, 3, 8), np.float32)
    for near in range(3):
        for token in range(16):
            source = token + near - 1
            if 0 <= source < 16:
                part = min(max(source - 1, 0) // STEP, PARTS - 1)
                for c in range(2):
                    for h in range(3):
                        out[near, c, h, token, part, c, h, source - part * STEP] = 1
    return out.reshape(3 * 96, 144)


def spreading():
    out = np.zeros((3, 2, 2, 2, LC, 2, 2, 2, 128), np.float32)
    for parity in range(2):
        for tap in range(3):
            column = parity + tap - 1
            near, b = 1 + column // 2, column % 2
            for pair in range(2):
                for a in range(2):
                    for ch in range(LC):
                        out[near, pair, a, b, ch, pair, a, parity, tap * LC + ch] = 1
    return out.reshape(3 * HD, 8 * 128)


def reordering():
    out = np.zeros((3, 16, 2, 2, 4, 2, 2, 4, 16), np.float32)
    for tap in range(3):
        for row in range(4):
            source = (row + tap + 1) // 2
            for frame in range(2):
                for parity in range(2):
                    for column in range(16):
                        out[tap, column, parity, frame, row, frame, parity, source, column] = 1
    return out.reshape(3, 256, 256)


def decode_kernel(
    clip_ref, place_ref, in_ref, table_ref, b_head_ref, w_in_ref, b_in_ref,
    gain_ref, w_up_ref, b_up_ref, out_ref,
):
    first_frame = 2 * place_ref[0]
    core = lax.rem(place_ref[0], 2)
    no_above = place_ref[1] == 0
    no_below = place_ref[1] == SEQ - 1
    total = in_ref[0].astype(jnp.float32)
    for g in range(1, GROUPS):
        total = total + in_ref[g].astype(jnp.float32)
    total = total + b_head_ref[...]
    total = total.reshape(144, HD)
    total = jnp.where(core == 0, pltpu.roll(total, LAT, 1), total)
    row = lax.broadcasted_iota(jnp.int32, (144, HD), 0)
    patch = lax.rem(lax.shift_right_logical(row, 3), 3)
    outside = ((patch == 0) & no_above) | ((patch == 2) & no_below)
    tokens = jnp.where(outside, 0.0, total).astype(jnp.bfloat16)
    gather = table_ref[768:1056, 0:144]
    tokens = jnp.dot(gather, tokens, preferred_element_type=jnp.float32)
    tokens = tokens.astype(jnp.bfloat16)
    near = jnp.concatenate([tokens[i * 96 : (i + 1) * 96] for i in range(3)], axis=1)
    cells = []
    for i in range(4):
        spread = table_ref[1056 + i * 384 : 1056 + (i + 1) * 384, :]
        cells.append(jnp.dot(near, spread, preferred_element_type=jnp.float32))
    cells = jnp.concatenate(cells, axis=1).astype(jnp.bfloat16)

    hidden = jnp.zeros((256, C1), jnp.float32)
    for time_tap in (2, 1, 0):
        part = jnp.zeros((256, C1), jnp.float32)
        for row_tap in range(3):
            pieces = []
            for f in range(2):
                pair, c = divmod(f + time_tap, 2)
                for parity in range(2):
                    for r in range(4):
                        h, a = divmod(r + row_tap, 2)
                        e = (pair * 2 + a) * 2 + parity
                        rows = slice((c * 3 + h) * 16, (c * 3 + h + 1) * 16)
                        pieces.append(cells[rows, e * 128 : e * 128 + 3 * LC])
            columns = jnp.concatenate(pieces, axis=0)
            tap = (time_tap * 3 + row_tap) * 3 * LC
            part = part + jnp.dot(
                columns, w_in_ref[tap : tap + 3 * LC, :], preferred_element_type=jnp.float32
            )
        if time_tap == 2:
            hidden = part + b_in_ref[...]
        else:
            kept = []
            for f in range(2):
                earlier = first_frame + (f + time_tap - 2)
                same = clip_ref[jnp.maximum(earlier, 0)] == clip_ref[first_frame + f]
                keep = (earlier >= 0) & same
                kept.append(jnp.where(keep, part[f * 128 : (f + 1) * 128], 0.0))
            hidden = hidden + jnp.concatenate(kept, axis=0)
    mean_square = jnp.mean(hidden * hidden, axis=-1, keepdims=True)
    normed = hidden * lax.rsqrt(mean_square + 1e-06) * gain_ref[...]
    active = normed / (1.0 + jnp.exp(-normed))
    row = lax.broadcasted_iota(jnp.int32, (256, C1), 0)
    grid_row = lax.bitwise_and(lax.shift_right_logical(row, 4), 3)
    outside = ((grid_row == 0) & no_above) | ((grid_row == 3) & no_below)
    active = jnp.where(outside, 0.0, active).astype(jnp.bfloat16)

    taps = [jnp.zeros((256, CO), jnp.float32) for _ in range(3)]
    for row_tap in range(3):
        order = table_ref[row_tap * 256 : (row_tap + 1) * 256, :]
        placed = jnp.dot(order, active, preferred_element_type=jnp.float32)
        placed = placed.astype(jnp.bfloat16)
        for col_tap in range(3):
            tap = (row_tap * 3 + col_tap) * C1
            taps[col_tap] = taps[col_tap] + lax.dot_general(
                placed, w_up_ref[:, tap : tap + C1], NT, preferred_element_type=jnp.float32
            )
    edge = jnp.zeros((8, CO), jnp.float32)
    before = jnp.concatenate([edge, taps[0][:-8]], axis=0)
    after = jnp.concatenate([taps[2][8:], edge], axis=0)
    even = before + taps[1] + taps[2] + b_up_ref[...]
    odd = taps[0] + taps[1] + after + b_up_ref[...]
    both = jnp.concatenate([even, odd], axis=1).astype(jnp.bfloat16).astype(jnp.float32)
    for column in range(32):
        piece = both[column * 8 : column * 8 + 8]
        lanes = slice(column * 2 * CO, (column + 1) * 2 * CO)
        out_ref[0, :, lanes] = piece[:4].astype(jnp.bfloat16)
        out_ref[1, :, lanes] = piece[4:].astype(jnp.bfloat16)


def decode(clip_ids, place, back, b_head, w_in, b_in, gain_in, w_up, b_up):
    vmem = pl.BlockSpec(memory_space=pltpu.VMEM)
    table = np.zeros((2592, 256), np.float32)
    table[:768] = reordering().reshape(768, 256)
    table[768:1056, :144] = assembly()
    table[1056:] = spreading().reshape(384, 4, 256).transpose(1, 0, 2).reshape(1536, 256)
    return pl.pallas_call(
        decode_kernel,
        in_specs=[pl.BlockSpec(memory_space=pltpu.SMEM)] * 2 + [vmem] * 8,
        out_specs=vmem,
        out_shape=jax.ShapeDtypeStruct((2, 4, 64 * CO), jnp.bfloat16),
        compiler_params=pltpu.CompilerParams(vmem_limit_bytes=12 * MIB),
    )(
        clip_ids,
        place,
        back,
        jnp.asarray(table, jnp.bfloat16),
        jnp.concatenate([b_head, b_head])[None],
        w_in,
        b_in[None],
        gain_in[None],
        w_up.T,
        b_up[None],
    )


def shards(queries, keys, values, clip_ids, w_head, b_head, w_in, b_in, gain_in, w_up, b_up):
    frame_position = lax.axis_index("frm")
    row_position = lax.axis_index("seq")
    core = lax.rem(frame_position, 2)

    slots = pack(queries, keys, values, w_head).reshape(FRM * SEQ, SLOT, HD)
    own = lax.all_to_all(slots, ("seq", "frm"), 0, 0, tiled=True)
    own_kv, own_q = prepare(own.reshape(SEQ, FRM, SLOT, HD))
    other_kv = lax.ppermute(own_kv, "frm", [(i, i ^ 1) for i in range(FRM)])

    below = jnp.sum(clip_ids[None, :] < clip_ids[:, None], axis=1, dtype=jnp.int32)
    upto = jnp.sum(clip_ids[None, :] <= clip_ids[:, None], axis=1, dtype=jnp.int32)
    kind = lax.broadcasted_iota(jnp.int32, (4, 2 * FRM), 0)
    meta = jnp.where(kind == 0, clip_ids, jnp.where(kind == 1, below, jnp.where(kind == 2, upto, core)))
    mixed = attend(meta, own_q, own_kv, other_kv)
    by_row = lax.all_to_all(mixed.reshape(SEQ, -1, HD), "seq", 0, 0, tiled=True)
    merged = merge(by_row.reshape(SEQ, 3, FRM // GATHER_F, GATHER_R, HD)).reshape(FRM, 24, HD)
    back = lax.all_to_all(merged, "frm", 0, 0, tiled=True)

    back = back[: 2 * PARTS * GROUPS].reshape(GROUPS, 2 * PARTS, 24, HD)
    place = jnp.where(jnp.arange(2) == 0, frame_position, row_position)
    return decode(clip_ids, place, back, b_head, w_in, b_in, gain_in, w_up, b_up)


def solution(mesh):
    in_specs = (
        P("frm", "seq", None),
        P("frm", "seq", None),
        P("frm", "seq", None),
        P(),
        P(),
        P(),
        P(),
        P(),
        P(),
        P(),
        P(),
    )
    out_specs = P("frm", "seq", None)
    return jax.shard_map(shards, mesh=mesh, in_specs=in_specs, out_specs=out_specs, check_vma=False)
```

```python
import functools
import math

import jax
import jax.numpy as jnp
import numpy as np
from jax import lax
from jax.experimental import pallas as pl
from jax.experimental.pallas import tpu as pltpu
from jax.sharding import PartitionSpec as P

HEADS = 40
HD = 128
LC = 16
C1 = 384
CO = 192
SEQ = 8
FRM = 32
GROUPS = 5
PARTS = 3
SHARE = 6
STEP = 5
SLOT = 32
LAT = 64
SPAN = SEQ * HD
FRAME_Q = SEQ * SHARE
GATHER_F = 8
GATHER_R = GATHER_F // 2 * SHARE
TILE_Q = 256
TILES = FRM * FRAME_Q // TILE_Q
TILE_SPAN = -(-TILE_Q // FRAME_Q) + 1
SIZES = (12, 17, 24, 32)
GROUP = 2
COEF = math.log2(math.e) / math.sqrt(HD)
FAR = -1e30
MIB = 1024 * 1024
NT = (((1,), (1,)), ((), ()))


def pack_kernel(q_hbm, k_hbm, v_hbm, w_hbm, out_ref, q_ref, k_ref, v_ref, w_ref, sems):
    copies = []
    for g in range(GROUPS):
        cols = slice(g * SPAN, (g + 1) * SPAN)
        group = []
        for i, (src, dst) in enumerate(
            ((v_hbm, v_ref), (k_hbm, k_ref), (q_hbm, q_ref), (w_hbm, w_ref))
        ):
            where = (slice(None), cols) if i == 3 else (slice(None), slice(None), cols)
            copy = pltpu.make_async_copy(src.at[where], dst.at[where], sems.at[g, i])
            copy.start()
            group.append(copy)
        copies.append(group)
    low = lax.broadcasted_iota(jnp.int32, (8, HD), 1) < LAT
    for g in range(GROUPS):
        for copy in copies[g]:
            copy.wait()
        for s in range(SEQ):
            cols = slice(g * SPAN + s * HD, g * SPAN + (s + 1) * HD)
            w = w_ref[:, cols]
            w2 = jnp.concatenate([w, w], axis=0)
            v = jnp.concatenate([v_ref[0, :, cols], v_ref[1, :, cols]], axis=0)
            proj = lax.dot_general(v, w2, NT, preferred_element_type=jnp.float32)
            keys = [k_ref[p, :, cols].astype(jnp.float32) for p in range(2)]
            for c in range(2):
                half = slice(c * 8, c * 8 + 8)
                k = jnp.concatenate([keys[0][half], keys[1][half]], axis=0).astype(jnp.bfloat16)
                packed = jnp.where(low, proj[c * 8 : c * 8 + 8], proj[16 + c * 8 : 24 + c * 8])
                q = q_ref[c, :, cols].astype(jnp.float32)
                for part in range(PARTS):
                    own = q if part == 0 else pltpu.roll(q, 16 - part * STEP, 0)
                    tail = jnp.concatenate([packed, own[:8]], axis=0)
                    out_ref[s, g * PARTS + part, c, 0:16, :] = k
                    out_ref[s, g * PARTS + part, c, 16:32, :] = tail.astype(jnp.bfloat16)


def pack(queries, keys, values, w_head):
    hbm = pl.BlockSpec(memory_space=pltpu.HBM)
    act = pltpu.VMEM((2, 16, HEADS * HD), jnp.bfloat16)
    return pl.pallas_call(
        pack_kernel,
        in_specs=[hbm, hbm, hbm, hbm],
        out_specs=pl.BlockSpec(memory_space=pltpu.VMEM),
        out_shape=pltpu.VMEM((SEQ, FRM // 2, 2, SLOT, HD), jnp.bfloat16),
        scratch_shapes=[
            act,
            act,
            act,
            pltpu.VMEM((LAT, HEADS * HD), jnp.bfloat16),
            pltpu.SemaphoreType.DMA((GROUPS, 4)),
        ],
        compiler_params=pltpu.CompilerParams(vmem_limit_bytes=12 * MIB),
    )(*(pltpu.with_memory_space_constraint(x, pltpu.HBM) for x in (queries, keys, values, w_head.T)))


def prepare_kernel(in_ref, kv_ref, q_ref, pick_ref):
    row = lax.broadcasted_iota(jnp.int32, (2 * FRAME_Q, 256), 0)
    col = lax.broadcasted_iota(jnp.int32, (2 * FRAME_Q, 256), 1)
    inner = lax.bitwise_and(col, 15) - 8
    hit = (row == SHARE * lax.shift_right_logical(col, 4) + inner) & (inner >= 0) & (inner < SHARE)
    pick_ref[...] = jnp.where(hit, 1.0, 0.0).astype(jnp.bfloat16)

    def body(i, carry):
        for j in range(2):
            f = 2 * i + j
            kv_ref[f, 0:128, :] = in_ref[:, f, 0:16, :].reshape(128, HD)
            packed = in_ref[:, f, 16:32, :].astype(jnp.float32)[:, :8]
            rolled = pltpu.roll(packed.reshape(SEQ * 8, HD), LAT, 1).reshape(SEQ, 8, HD)
            block = jnp.concatenate([packed, rolled], axis=1).reshape(128, HD).T
            kv_ref[f, 128:192, :] = block[:LAT].astype(jnp.bfloat16)
        q = [in_ref[:, 2 * i + j, 16:32, :].reshape(128, HD) for j in range(2)]
        q = jnp.concatenate(q, axis=0)
        q = jnp.dot(pick_ref[...], q, preferred_element_type=jnp.float32)
        rows = pl.multiple_of(i * 2 * FRAME_Q, 2 * FRAME_Q)
        q_ref[pl.ds(rows, 2 * FRAME_Q), :] = q.astype(jnp.bfloat16)
        return carry

    lax.fori_loop(0, FRM // 2, body, 0, unroll=16)


def prepare(own):
    vmem = pl.BlockSpec(memory_space=pltpu.VMEM)
    return pl.pallas_call(
        prepare_kernel,
        in_specs=[vmem],
        out_specs=[vmem, vmem],
        out_shape=[
            pltpu.VMEM((FRM, 128 + LAT, HD), jnp.bfloat16),
            pltpu.VMEM((FRM * FRAME_Q, HD), jnp.bfloat16),
        ],
        scratch_shapes=[pltpu.VMEM((2 * FRAME_Q, 256), jnp.bfloat16)],
        compiler_params=pltpu.CompilerParams(vmem_limit_bytes=12 * MIB),
    )(own)


def attend_kernel(meta_ref, q_ref, own_ref, other_ref, out_ref, s_ref, done_ref, place_ref):
    core = meta_ref[3, 0]
    share = lax.broadcasted_iota(jnp.int32, (SEQ * GATHER_R, 1), 0)
    source = jnp.zeros_like(share)
    for size, unit, stop in ((GATHER_R, SHARE, SEQ), (SHARE, FRAME_Q, GATHER_F // 2)):
        count = jnp.zeros_like(share)
        for i in range(1, stop):
            count = count + jnp.where(share >= size * i, 1, 0)
        share = share - count * size
        source = source + count * unit
    col = lax.broadcasted_iota(jnp.int32, (SEQ * GATHER_R, SEQ * GATHER_R), 1)
    place_ref[...] = jnp.where(col == source + share, 1.0, 0.0).astype(jnp.bfloat16)
    ones = jnp.ones((16, FRM * 128), jnp.bfloat16)
    lane = lax.broadcasted_iota(jnp.int32, (8, TILE_Q), 1)

    def setup(t):
        rows = pl.multiple_of(t * TILE_Q, TILE_Q)
        q = q_ref[pl.ds(rows, TILE_Q), :]
        begin_f = lax.div(rows, FRAME_Q)
        end_f = lax.div(rows + (TILE_Q - 1), FRAME_Q)
        first = lax.shift_right_logical(meta_ref[1, 2 * begin_f + core], 1)
        last = lax.shift_right_logical(meta_ref[2, 2 * end_f + core] + 1, 1)
        q_clip = jnp.zeros((8, TILE_Q), jnp.int32)
        for j in range(TILE_SPAN):
            f = begin_f + j
            clip = meta_ref[0, jnp.minimum(2 * f + core, 2 * FRM - 1)]
            q_clip = jnp.where(lane + rows >= f * FRAME_Q, clip, q_clip)
        return rows, q, q_clip, first, last - first

    def score(size, q, q_clip, first, buffer):
        start = jnp.minimum(first, FRM - size)
        top = jnp.full((8, TILE_Q), FAR, jnp.float32)
        biases = []
        for j in range(size):
            pair = []
            for p in range(2):
                clip = meta_ref[0, 2 * (start + j) + p]
                pair.append(jnp.where(q_clip == clip, 0.0, FAR))
            biases.append(jnp.concatenate(pair, axis=0)[None])
        for side, ref in enumerate((own_ref, other_ref)):
            k = ref[pl.ds(start, size), 0:128, :].reshape(size * 128, HD)
            s = lax.dot_general(k, q, NT, preferred_element_type=jnp.float32)
            for j in range(size):
                part = s[j * 128 : (j + 1) * 128].reshape(SEQ, 16, TILE_Q) + biases[j]
                buffer[side, j * 128 : (j + 1) * 128, :] = part.reshape(128, TILE_Q)
                top = jnp.maximum(top, jnp.max(part.reshape(16, 8, TILE_Q), axis=0))
        return top

    def mix(size, first, top, buffer):
        start = jnp.minimum(first, FRM - size)
        total = jnp.zeros((LAT + 16, TILE_Q), jnp.float32)
        for side, ref in enumerate((own_ref, other_ref)):
            weights = jnp.exp2((buffer[side, : size * 128] - top) * COEF).astype(jnp.bfloat16)
            vt = [ref[start + j, 128 : 128 + LAT, :] for j in range(size)]
            vt = jnp.concatenate([jnp.concatenate(vt, axis=1), ones[:, : size * 128]], axis=0)
            total = total + jnp.dot(vt, weights, preferred_element_type=jnp.float32)
        return total

    def store(rows, total):
        mixed = total[:LAT] / total[LAT : LAT + 1]
        done_ref[pl.ds(rows, TILE_Q), :] = jnp.concatenate([mixed, mixed], axis=0).T

    def pair(i, carry):
        tiles = [setup(GROUP * i + n) for n in range(GROUP)]
        widest = tiles[0][4]
        for n in range(1, GROUP):
            widest = jnp.maximum(widest, tiles[n][4])

        def together(size):
            tops = []
            for n, (rows, q, q_clip, first, span) in enumerate(tiles):
                top = score(size, q, q_clip, first, s_ref.at[n])
                tops.append(jnp.max(top, axis=0, keepdims=True))
            for n, (rows, q, q_clip, first, span) in enumerate(tiles):
                store(rows, mix(size, first, tops[n], s_ref.at[n]))

        for below, size in zip((0,) + SIZES, SIZES):
            fits = (widest > below) & (widest <= size)
            pl.when(fits)(functools.partial(together, size))
        return carry

    lax.fori_loop(0, TILES // GROUP, pair, 0)

    wide_low = lax.broadcasted_iota(jnp.int32, (FRAME_Q, HD), 1) < LAT
    for i in range(FRM // GATHER_F):
        packed = []
        for j in range(GATHER_F // 2):
            even = (i * GATHER_F + 2 * j) * FRAME_Q
            odd = even + FRAME_Q
            packed.append(
                jnp.where(wide_low, done_ref[even:odd, :], done_ref[odd : odd + FRAME_Q, :])
            )
        packed = jnp.concatenate(packed, axis=0).astype(jnp.bfloat16)
        placed = jnp.dot(place_ref[...], packed, preferred_element_type=jnp.float32)
        for s in range(SEQ):
            piece = placed[s * GATHER_R : (s + 1) * GATHER_R].astype(jnp.bfloat16)
            for halo in range(3):
                owner = s + 1 - halo
                if 0 <= owner < SEQ:
                    out_ref[owner, halo, i] = piece


def attend(meta, q, own, other):
    vmem = pl.BlockSpec(memory_space=pltpu.VMEM)
    return pl.pallas_call(
        attend_kernel,
        in_specs=[
            pl.BlockSpec(memory_space=pltpu.SMEM),
            vmem,
            vmem,
            vmem,
        ],
        out_specs=vmem,
        out_shape=pltpu.VMEM((SEQ, 3, FRM // GATHER_F, GATHER_R, HD), jnp.bfloat16),
        scratch_shapes=[
            pltpu.VMEM((GROUP, 2, FRM * 128, TILE_Q), jnp.float32),
            pltpu.VMEM((FRM * FRAME_Q, HD), jnp.float32),
            pltpu.VMEM((SEQ * GATHER_R, SEQ * GATHER_R), jnp.bfloat16),
        ],
        compiler_params=pltpu.CompilerParams(vmem_limit_bytes=36 * MIB),
    )(meta, q, own, other)


def merge_kernel(in_ref, w_in_ref, out_ref):
    low = lax.broadcasted_iota(jnp.int32, (FRM // 2, 8, HD), 2) < LAT
    row = lax.broadcasted_iota(jnp.int32, (FRM // 2 * 8, FRM // 2 * SHARE), 0)
    col = lax.broadcasted_iota(jnp.int32, (FRM // 2 * 8, FRM // 2 * SHARE), 1)
    share = lax.bitwise_and(row, 7)
    hit = (col == SHARE * lax.shift_right_logical(row, 3) + share) & (share < SHARE)
    widen = jnp.where(hit, 1.0, 0.0).astype(jnp.bfloat16)
    for halo in range(3):
        total = in_ref[0, halo].astype(jnp.float32)
        for head in range(1, SEQ):
            total = total + in_ref[head, halo].astype(jnp.float32)
        total = total.reshape(FRM // 2 * SHARE, HD).astype(jnp.bfloat16)
        total = jnp.dot(widen, total, preferred_element_type=jnp.float32)
        total = total.reshape(FRM // 2, 8, HD)
        before = jnp.concatenate([total[:1], total[:-1]], axis=0)
        out_ref[:, 0, halo] = jnp.where(low, total, before).astype(jnp.bfloat16)
        out_ref[:, 1, halo] = total.astype(jnp.bfloat16)


def merge(parts, w_in):
    vmem = pl.BlockSpec(memory_space=pltpu.VMEM)
    return pl.pallas_call(
        merge_kernel,
        in_specs=[vmem, vmem],
        out_specs=vmem,
        out_shape=pltpu.VMEM((FRM // 2, 2, 3, 8, HD), jnp.bfloat16),
        compiler_params=pltpu.CompilerParams(vmem_limit_bytes=12 * MIB),
    )(parts, w_in)


def assembly():
    out = np.zeros((3, 2, 3, 16, PARTS, 2, 3, 8), np.float32)
    for near in range(3):
        for token in range(16):
            source = token + near - 1
            if 0 <= source < 16:
                part = min(max(source - 1, 0) // STEP, PARTS - 1)
                for c in range(2):
                    for h in range(3):
                        out[near, c, h, token, part, c, h, source - part * STEP] = 1
    return out.reshape(3 * 96, 144)


def spreading():
    out = np.zeros((3, 2, 2, 2, LC, 2, 2, 2, 128), np.float32)
    for parity in range(2):
        for tap in range(3):
            column = parity + tap - 1
            near, b = 1 + column // 2, column % 2
            for pair in range(2):
                for a in range(2):
                    for ch in range(LC):
                        out[near, pair, a, b, ch, pair, a, parity, tap * LC + ch] = 1
    return out.reshape(3 * HD, 8 * 128)


def reordering():
    out = np.zeros((3, 16, 2, 2, 4, 2, 2, 4, 16), np.float32)
    for tap in range(3):
        for row in range(4):
            source = (row + tap + 1) // 2
            for frame in range(2):
                for parity in range(2):
                    for column in range(16):
                        out[tap, column, parity, frame, row, frame, parity, source, column] = 1
    return out.reshape(3, 256, 256)


def decode_kernel(
    clip_ref, place_ref, in_ref, table_ref, b_head_ref, w_in_ref, b_in_ref,
    gain_ref, w_up_ref, b_up_ref, out_ref,
):
    first_frame = 2 * place_ref[0]
    core = lax.rem(place_ref[0], 2)
    no_above = place_ref[1] == 0
    no_below = place_ref[1] == SEQ - 1
    total = in_ref[0].astype(jnp.float32)
    for g in range(1, GROUPS):
        total = total + in_ref[g].astype(jnp.float32)
    total = total + b_head_ref[...]
    total = total.reshape(144, HD)
    total = jnp.where(core == 0, pltpu.roll(total, LAT, 1), total)
    row = lax.broadcasted_iota(jnp.int32, (144, HD), 0)
    patch = lax.rem(lax.shift_right_logical(row, 3), 3)
    outside = ((patch == 0) & no_above) | ((patch == 2) & no_below)
    tokens = jnp.where(outside, 0.0, total).astype(jnp.bfloat16)
    gather = table_ref[768:1056, 0:144]
    tokens = jnp.dot(gather, tokens, preferred_element_type=jnp.float32)
    tokens = tokens.astype(jnp.bfloat16)
    near = jnp.concatenate([tokens[i * 96 : (i + 1) * 96] for i in range(3)], axis=1)
    cells = []
    for i in range(4):
        spread = table_ref[1056 + i * 384 : 1056 + (i + 1) * 384, :]
        cells.append(jnp.dot(near, spread, preferred_element_type=jnp.float32))
    cells = jnp.concatenate(cells, axis=1).astype(jnp.bfloat16)

    hidden = jnp.zeros((256, C1), jnp.float32)
    for time_tap in (2, 1, 0):
        part = jnp.zeros((256, C1), jnp.float32)
        for row_tap in range(3):
            pieces = []
            for f in range(2):
                pair, c = divmod(f + time_tap, 2)
                for parity in range(2):
                    for r in range(4):
                        h, a = divmod(r + row_tap, 2)
                        e = (pair * 2 + a) * 2 + parity
                        rows = slice((c * 3 + h) * 16, (c * 3 + h + 1) * 16)
                        pieces.append(cells[rows, e * 128 : e * 128 + 3 * LC])
            columns = jnp.concatenate(pieces, axis=0)
            tap = (time_tap * 3 + row_tap) * 3 * LC
            part = part + jnp.dot(
                columns, w_in_ref[tap : tap + 3 * LC, :], preferred_element_type=jnp.float32
            )
        if time_tap == 2:
            hidden = part + b_in_ref[...]
        else:
            kept = []
            for f in range(2):
                earlier = first_frame + (f + time_tap - 2)
                same = clip_ref[jnp.maximum(earlier, 0)] == clip_ref[first_frame + f]
                keep = (earlier >= 0) & same
                kept.append(jnp.where(keep, part[f * 128 : (f + 1) * 128], 0.0))
            hidden = hidden + jnp.concatenate(kept, axis=0)
    mean_square = jnp.mean(hidden * hidden, axis=-1, keepdims=True)
    normed = hidden * lax.rsqrt(mean_square + 1e-06) * gain_ref[...]
    active = normed / (1.0 + jnp.exp(-normed))
    row = lax.broadcasted_iota(jnp.int32, (256, C1), 0)
    grid_row = lax.bitwise_and(lax.shift_right_logical(row, 4), 3)
    outside = ((grid_row == 0) & no_above) | ((grid_row == 3) & no_below)
    active = jnp.where(outside, 0.0, active).astype(jnp.bfloat16)

    taps = [jnp.zeros((256, CO), jnp.float32) for _ in range(3)]
    for row_tap in range(3):
        order = table_ref[row_tap * 256 : (row_tap + 1) * 256, :]
        placed = jnp.dot(order, active, preferred_element_type=jnp.float32)
        placed = placed.astype(jnp.bfloat16)
        for col_tap in range(3):
            tap = (row_tap * 3 + col_tap) * C1
            taps[col_tap] = taps[col_tap] + lax.dot_general(
                placed, w_up_ref[:, tap : tap + C1], NT, preferred_element_type=jnp.float32
            )
    edge = jnp.zeros((8, CO), jnp.float32)
    before = jnp.concatenate([edge, taps[0][:-8]], axis=0)
    after = jnp.concatenate([taps[2][8:], edge], axis=0)
    even = before + taps[1] + taps[2] + b_up_ref[...]
    odd = taps[0] + taps[1] + after + b_up_ref[...]
    both = jnp.concatenate([even, odd], axis=1).astype(jnp.bfloat16).astype(jnp.float32)
    for column in range(32):
        piece = both[column * 8 : column * 8 + 8]
        lanes = slice(column * 2 * CO, (column + 1) * 2 * CO)
        out_ref[0, :, lanes] = piece[:4].astype(jnp.bfloat16)
        out_ref[1, :, lanes] = piece[4:].astype(jnp.bfloat16)


def decode(clip_ids, place, back, b_head, w_in, b_in, gain_in, w_up, b_up):
    vmem = pl.BlockSpec(memory_space=pltpu.VMEM)
    table = np.zeros((2592, 256), np.float32)
    table[:768] = reordering().reshape(768, 256)
    table[768:1056, :144] = assembly()
    table[1056:] = spreading().reshape(384, 4, 256).transpose(1, 0, 2).reshape(1536, 256)
    return pl.pallas_call(
        decode_kernel,
        in_specs=[pl.BlockSpec(memory_space=pltpu.SMEM)] * 2 + [vmem] * 8,
        out_specs=vmem,
        out_shape=jax.ShapeDtypeStruct((2, 4, 64 * CO), jnp.bfloat16),
        compiler_params=pltpu.CompilerParams(vmem_limit_bytes=12 * MIB),
    )(
        clip_ids,
        place,
        back,
        jnp.asarray(table, jnp.bfloat16),
        jnp.concatenate([b_head, b_head])[None],
        w_in,
        b_in[None],
        gain_in[None],
        w_up.T,
        b_up[None],
    )


def shards(queries, keys, values, clip_ids, w_head, b_head, w_in, b_in, gain_in, w_up, b_up):
    frame_position = lax.axis_index("frm")
    row_position = lax.axis_index("seq")
    core = lax.rem(frame_position, 2)

    slots = pack(queries, keys, values, w_head).reshape(FRM * SEQ, SLOT, HD)
    own = lax.all_to_all(slots, ("seq", "frm"), 0, 0, tiled=True)
    own_kv, own_q = prepare(own.reshape(SEQ, FRM, SLOT, HD))
    other_kv = lax.ppermute(own_kv, "frm", [(i, i ^ 1) for i in range(FRM)])

    below = jnp.sum(clip_ids[None, :] < clip_ids[:, None], axis=1, dtype=jnp.int32)
    upto = jnp.sum(clip_ids[None, :] <= clip_ids[:, None], axis=1, dtype=jnp.int32)
    kind = lax.broadcasted_iota(jnp.int32, (4, 2 * FRM), 0)
    meta = jnp.where(kind == 0, clip_ids, jnp.where(kind == 1, below, jnp.where(kind == 2, upto, core)))
    mixed = attend(meta, own_q, own_kv, other_kv)
    by_row = lax.all_to_all(mixed.reshape(SEQ, -1, HD), "seq", 0, 0, tiled=True)
    merged = merge(by_row.reshape(SEQ, 3, FRM // GATHER_F, GATHER_R, HD), w_in).reshape(FRM, 24, HD)
    back = lax.all_to_all(merged, "frm", 0, 0, tiled=True)

    back = back[: 2 * PARTS * GROUPS].reshape(GROUPS, 2 * PARTS, 24, HD)
    place = jnp.where(jnp.arange(2) == 0, frame_position, row_position)
    return decode(clip_ids, place, back, b_head, w_in, b_in, gain_in, w_up, b_up)


def solution(mesh):
    in_specs = (
        P("frm", "seq", None),
        P("frm", "seq", None),
        P("frm", "seq", None),
        P(),
        P(),
        P(),
        P(),
        P(),
        P(),
        P(),
        P(),
    )
    out_specs = P("frm", "seq", None)
    return jax.shard_map(shards, mesh=mesh, in_specs=in_specs, out_specs=out_specs, check_vma=False)
```
